256 devices in a mesh: cfg: 2 (over core), section: 8 (over y, x_hi), patch: 16 (over z, x_lo).
Axes of the slice: x: 4 (x_hi: 2, x_lo: 2; x = x_hi * 2 + x_lo), y: 4, z: 8, core: 2. Of those that a mesh axis runs over, the one named last changes fastest.
Arguments:
- hidden_in: float32 [2, 8, 640, 2432], P('cfg', 'section', 'patch'), may hold values from -12 to 12, as said below
- latent_in: float32 [8, 640, 64], P('section', 'patch'), may hold values from -6 to 6
- kv_cache: bfloat16 [2, 8, 5120, 2, 2048], P('cfg', 'section', None, None, 'patch'), may hold values from -6 to 6
- text_kv: bfloat16 [2, 8, 333, 2, 2048], P('cfg', 'section', None, None, 'patch'), may hold values from -6 to 6
- qkv_weight: bfloat16 [8, 2432, 3, 2048], P('section', None, None, 'patch'), may hold values from -0.125 to 0.125
- out_weight: bfloat16 [8, 2048, 2432], P('section', 'patch'), may hold values from -0.75 to 0.75
- mod_table: float32 [8, 28, 3, 2432], P('section'), may hold values from -4 to 4
- final_mod: float32 [28, 2, 2432], replicated, may hold values from -3 to 3
- final_weight: bfloat16 [2432, 64], replicated, may hold values from -0.125 to 0.125
- embed_weight: bfloat16 [64, 2432], replicated, may hold values from -0.75 to 0.75
- pos_embed: bfloat16 [8, 640, 2432], P(None, 'patch'), may hold values from -6 to 6
- patch_order: int32 [8], replicated, may hold values from 0 to 7, each once
- step_index: int32 [1], replicated, may hold values from 0 to 26
- guidance: int32 [1], replicated, may hold values from 192 to 384
Outputs:
- hidden_out: float32 [2, 8, 640, 2432], P('cfg', 'section', 'patch')
- latent_out: float32 [8, 640, 64], P('section', 'patch')
The draws below stay inside these ranges and needn't reach their ends.
Inputs may be any that keep to these rules, and one draw needn't show every extreme that they name: `hidden_in`: each row and each feature column is scaled by a factor between e^-1.15 and e^1.15; columns may carry a nonzero mean. `patch_order`: each patch number once.
All inputs are finite; a program needn't handle non-finite values.
Results may differ from the reference program's by a relative error of at most 0.0085.
Values may be sent and summed in bfloat16 or wider, within the bound.
No kernel may reach another device: no remote copies, remote signals or barrier semaphores. Data moves between devices by JAX's collectives and lax.ppermute only.
A program may use at most 128 MiB of HBM per device.

```python
import jax
import jax.numpy as jnp
from jax import lax

D = 2432
HEADS = 32
HEAD = 64
CHAN = 64
TXT = 333
NT = 28
TICKS = 2
NP = 8
PTOK = 640
LEN = 5120
HH = 2048


def draw_hidden_in(key, part):
    key = jax.random.fold_in(key, 11)
    key_base, key_cols, key_rows = jax.random.split(key, 3)
    draw_shape = (2, NP, PTOK, D)
    col_scale = jnp.exp(jax.random.uniform(key_cols, (1, 1, 1, D), jnp.float32, -1.15, 1.15))
    row_scale = jnp.exp(jax.random.uniform(key_rows, (2, NP, PTOK, 1), jnp.float32, -1.15, 1.15))
    base_part = jnp.clip(jax.random.normal(key_base, draw_shape, jnp.float32), -4.5, 4.5)
    return 0.25 * base_part * col_scale * row_scale


def level_of(key, extent, shards, smallest, largest):
    factor_of, own = 1.0, jax.random.fold_in(key, 6)
    for axis_at, parts in shards:
        steps = jnp.exp(jax.random.uniform(jax.random.fold_in(own, axis_at), (parts,), jnp.float32, smallest / len(shards), largest / len(shards)))
        factor_of = factor_of * jnp.repeat(steps, extent[axis_at] // parts).reshape([-1 if axis == axis_at else 1 for axis in range(len(extent))])
    return factor_of


def normal_values(key, dims, deviation, bound, pieces=(), held_as=jnp.bfloat16):
    factor_of = level_of(key, dims, pieces, -0.22, 0.18) if pieces else 1.0
    drawn = jax.random.normal(key, dims, jnp.float32) * deviation * factor_of
    return jnp.minimum(jnp.maximum(drawn, -bound), bound).astype(held_as)


def setup_inputs(seed: int = 0) -> dict:
    key_of = jax.random.split(jax.random.key(seed), 15)
    hidden_in = draw_hidden_in(jax.random.fold_in(key_of[14], 71), 0)
    latent_in = normal_values(key_of[1], (NP, PTOK, CHAN), 1.0, 6.0, ((0, 8), (1, 16)), jnp.float32)
    kv_cache = normal_values(key_of[2], (2, NP, LEN, 2, HH), 1.0, 6.0, ((0, 2), (1, 8), (4, 16)))
    text_kv = normal_values(key_of[3], (2, NP, TXT, 2, HH), 1.0, 6.0, ((0, 2), (1, 8), (4, 16)))
    qkv_weight = normal_values(key_of[4], (NP, D, 3, HH), D ** -0.5, 0.125, ((0, 8), (3, 16)))
    out_weight = normal_values(key_of[5], (NP, HH, D), HEAD ** -0.5, 0.75, ((0, 8), (1, 16)))
    mod_table = normal_values(key_of[6], (NP, NT, 3, D), 1.0, 4.0, ((0, 8),), jnp.float32)
    final_mod = normal_values(key_of[7], (NT, 2, D), 0.5, 3.0, (), jnp.float32)
    final_weight = normal_values(key_of[8], (D, CHAN), D ** -0.5, 0.125)
    embed_weight = normal_values(key_of[9], (CHAN, D), CHAN ** -0.5, 0.75)
    pos_embed = normal_values(key_of[10], (NP, PTOK, D), 1.0, 6.0, ((1, 16),))
    patch_order = jax.random.permutation(key_of[11], NP).astype(jnp.int32)
    step_index = jax.random.randint(key_of[12], (1,), 0, NT - 1).astype(jnp.int32)
    guidance = jax.random.randint(key_of[13], (1,), 192, 385).astype(jnp.int32)
    return {"hidden_in": hidden_in, "latent_in": latent_in, "kv_cache": kv_cache, "text_kv": text_kv, "qkv_weight": qkv_weight, "out_weight": out_weight, "mod_table": mod_table, "final_mod": final_mod, "final_weight": final_weight, "embed_weight": embed_weight, "pos_embed": pos_embed, "patch_order": patch_order, "step_index": step_index, "guidance": guidance}


EPSILON = 1e-06

def sigma_of(time_level):
    frac = 1.0 - time_level.astype(jnp.float32) / NT
    return 3.0 * frac / (1.0 + 2.0 * frac)

def layer_norm(values):
    center = values - lax.optimization_barrier(jnp.mean(values, axis=-1, keepdims=True))
    return center / jnp.sqrt(lax.optimization_barrier(jnp.mean(center * center, axis=-1, keepdims=True)) + EPSILON)

def head_norm(values):
    shaped = values.reshape(values.shape[0], -1, HEAD)
    scaled = shaped / jnp.sqrt(lax.optimization_barrier(jnp.mean(shaped * shaped, axis=-1, keepdims=True)) + EPSILON)
    return scaled.reshape(values.shape[0], -1).astype(jnp.bfloat16)

def attend(queries, key_rows, value_rows):

    def one_head(head_id):
        first_col = head_id * HEAD
        query_head = lax.dynamic_slice_in_dim(queries, first_col, HEAD, 1)
        key_head = lax.dynamic_slice_in_dim(key_rows, first_col, HEAD, 1)
        value_head = lax.dynamic_slice_in_dim(value_rows, first_col, HEAD, 1)
        scores = jnp.dot(query_head, key_head.T, preferred_element_type=jnp.float32) * HEAD ** (-0.5)
        expscore = jnp.exp(scores)
        row_total = lax.optimization_barrier(jnp.sum(expscore, axis=1, keepdims=True))
        weights = expscore.astype(jnp.bfloat16)
        summed = jnp.dot(weights, value_head, preferred_element_type=jnp.float32)
        return (summed / row_total).astype(jnp.bfloat16)
    stacked = lax.map(one_head, jnp.arange(HEADS, dtype=jnp.int32))
    return jnp.transpose(stacked, (1, 0, 2)).reshape(queries.shape[0], HEADS * HEAD)

def reference(hidden_in, latent_in, kv_cache, text_kv, qkv_weight, out_weight, mod_table, final_mod, final_weight, embed_weight, pos_embed, patch_order, step_index, guidance):
    sections = NP
    width_all = HEADS * HEAD
    hidden = [[hidden_in[branch, section_id] for section_id in range(sections)] for branch in range(2)]
    latent = [latent_in[section_id] for section_id in range(sections)]
    caches = [[kv_cache[branch, section_id] for section_id in range(sections)] for branch in range(2)]
    guide_scale = guidance[0].astype(jnp.float32) / 64.0
    for window_tick in range(TICKS):
        updated = [[None] * sections for branch in range(2)]
        levels = []
        patches = []
        for section_id in range(sections):
            position = NP - 1 + window_tick - section_id
            offset = 1 if position >= NP else 0
            patch_id = patch_order[position % NP]
            time_level = step_index[0] + offset
            levels.append(time_level)
            patches.append(patch_id)
            modulation = lax.dynamic_index_in_dim(mod_table[section_id], time_level, 0, keepdims=False)
            for branch in range(2):
                hidden_rows = hidden[branch][section_id]
                normed = (layer_norm(hidden_rows) * (1.0 + modulation[1]) + modulation[0]).astype(jnp.bfloat16)
                mixed_rows = jnp.dot(normed, qkv_weight[section_id].reshape(D, 3 * width_all), preferred_element_type=jnp.float32).reshape(PTOK, 3, width_all)
                queries = head_norm(mixed_rows[:, 0])
                key_new = head_norm(mixed_rows[:, 1])
                value_new = mixed_rows[:, 2].astype(jnp.bfloat16)
                fresh = jnp.stack([key_new, value_new], axis=1)
                kv_store = lax.dynamic_update_slice_in_dim(caches[branch][section_id], fresh, (patch_id * PTOK).astype(jnp.int32), 0)
                caches[branch][section_id] = kv_store
                all_keys = jnp.concatenate([text_kv[branch, section_id][:, 0], kv_store[:, 0]], axis=0)
                all_values = jnp.concatenate([text_kv[branch, section_id][:, 1], kv_store[:, 1]], axis=0)
                attended = attend(queries, all_keys, all_values)
                projected = jnp.dot(attended, out_weight[section_id], preferred_element_type=jnp.float32)
                updated[branch][section_id] = hidden_rows + modulation[2] * projected
        last_section = sections - 1
        time_level = levels[last_section]
        final_mods = lax.dynamic_index_in_dim(final_mod, time_level, 0, keepdims=False)
        velocity = []
        for branch in range(2):
            final_normed = (layer_norm(updated[branch][last_section]) * (1.0 + final_mods[1]) + final_mods[0]).astype(jnp.bfloat16)
            velocity.append(jnp.dot(final_normed, final_weight, preferred_element_type=jnp.float32))
        guided = velocity[1] + guide_scale * (velocity[0] - velocity[1])
        new_latent = latent[last_section] + (sigma_of(time_level + 1) - sigma_of(time_level)) * guided
        position_rows = lax.dynamic_index_in_dim(pos_embed, patches[last_section], 0, keepdims=False).astype(jnp.float32)
        embedded = jnp.dot(new_latent.astype(jnp.bfloat16), embed_weight, preferred_element_type=jnp.float32) + position_rows
        hidden = [[embedded] + updated[branch][:last_section] for branch in range(2)]
        latent = [new_latent] + latent[:last_section]
    hidden_out = jnp.stack([jnp.stack(hidden[branch]) for branch in range(2)])
    latent_out = jnp.stack(latent)
    return (hidden_out, latent_out)
```

```python
import math

import jax
import jax.numpy as jnp
from jax import lax
from jax.experimental import pallas as pl
from jax.experimental.pallas import tpu as pltpu
from jax.sharding import PartitionSpec as P

HEAD = 64
NT = 28
TICKS = 2
EPSILON = 1e-06
BF = jnp.bfloat16
F32 = jnp.float32
VMEM_LIMIT = 48 * 1024 * 1024
Q_SCALE = math.log2(math.e) / math.sqrt(HEAD)
GROUPS = ((0, 1, -1, 2, -2, 3, -3, 4),)
LANES = 128
TEXT_PAD = 384


def params():
    return pltpu.CompilerParams(vmem_limit_bytes=VMEM_LIMIT)


def cost(flops, moved, exps=0):
    return pl.CostEstimate(flops=int(flops), bytes_accessed=int(moved), transcendentals=int(exps))


def sigma_of(time_level):
    frac = 1.0 - time_level.astype(F32) / NT
    return 3.0 * frac / (1.0 + 2.0 * frac)


def normalize(values):
    center = values - jnp.mean(values, axis=-1, keepdims=True)
    return center / jnp.sqrt(jnp.mean(center * center, axis=-1, keepdims=True) + EPSILON)


def norm_rows(hidden, mod_table, level):
    rows, width = hidden.shape

    def kernel(level_ref, hidden_ref, mod_ref, out_ref):
        values = normalize(hidden_ref[...].astype(F32))
        out_ref[...] = (values * (1.0 + mod_ref[0, 1:2]) + mod_ref[0, 0:1]).astype(BF)

    return pl.pallas_call(
        kernel,
        out_shape=jax.ShapeDtypeStruct((rows, width), BF),
        grid_spec=pltpu.PrefetchScalarGridSpec(
            num_scalar_prefetch=1,
            grid=(1,),
            in_specs=[
                pl.BlockSpec((rows, width), lambda i, lv: (0, 0)),
                pl.BlockSpec((1, 3, width), lambda i, lv: (lv[0], 0, 0)),
            ],
            out_specs=pl.BlockSpec((rows, width), lambda i, lv: (0, 0)),
        ),
        compiler_params=params(),
        cost_estimate=cost(10 * rows * width, 6 * rows * width),
        name="norm_rows",
    )(level, hidden, mod_table)


def head_scale(values, factor):
    lane = lax.broadcasted_iota(jnp.int32, values.shape, 1)
    square = values * values
    low = jnp.sum(jnp.where(lane < HEAD, square, 0.0), axis=1, keepdims=True)
    high = jnp.sum(jnp.where(lane < HEAD, 0.0, square), axis=1, keepdims=True)
    total = jnp.where(lane < HEAD, low, high)
    return values * (factor / jnp.sqrt(total * (1.0 / HEAD) + EPSILON))


def project(chunks, weight):
    count = len(chunks)
    rows, width = chunks[0].shape
    total = count * rows
    wide = weight.shape[1]

    def kernel(*refs):
        chunk_refs, (weight_ref, own_ref, other_ref, gathered) = refs[:count], refs[count:]
        for at, ref in enumerate(chunk_refs):
            gathered[at * rows : (at + 1) * rows, :] = ref[...].astype(F32)
        mixed = jnp.dot(gathered[...].astype(BF), weight_ref[...], preferred_element_type=F32)
        for out_ref, first in ((own_ref, 0), (other_ref, 3 * LANES)):
            part = mixed[:, first : first + 3 * LANES]
            out_ref[:, 0:LANES] = head_scale(part[:, 0:LANES], Q_SCALE).astype(BF)
            out_ref[:, LANES : 2 * LANES] = head_scale(part[:, LANES : 2 * LANES], 1.0).astype(BF)
            out_ref[:, 2 * LANES :] = part[:, 2 * LANES :].astype(BF)

    return pl.pallas_call(
        kernel,
        out_shape=[jax.ShapeDtypeStruct((total, 3 * LANES), BF)] * 2,
        in_specs=[pl.BlockSpec(memory_space=pltpu.VMEM)] * (count + 1),
        out_specs=[pl.BlockSpec(memory_space=pltpu.VMEM)] * 2,
        scratch_shapes=[pltpu.VMEM((total, width), F32)],
        compiler_params=params(),
        cost_estimate=cost(2 * total * width * wide, 2 * wide * width + 2 * total * width),
        name="project",
    )(*chunks, weight)


def masked_queries(queries):
    lane = lax.broadcasted_iota(jnp.int32, queries.shape, 1)
    zero = jnp.zeros_like(queries)
    return jnp.where(lane < HEAD, queries, zero), jnp.where(lane < HEAD, zero, queries)


def weigh(query, keys, values):
    scores = lax.dot_general(
        query, keys, (((1,), (1,)), ((), ())), preferred_element_type=F32
    )
    return jnp.dot(jnp.exp2(scores).astype(BF), values, preferred_element_type=F32)


def with_ones(values):
    return jnp.concatenate([values, jnp.ones(values.shape, BF)], axis=1)


def attend_stale(order, own, recv, keys, values, text_keys, text_values, fresh):
    rows = own.shape[0]
    patch_rows = keys.shape[1]
    blocks = order.shape[0]
    extra = len(fresh)

    def kernel(order_ref, own_ref, recv_ref, key_ref, value_ref, text_key_ref, text_value_ref, *rest):
        fresh_refs, acc_ref = rest[:extra], rest[extra]
        step = pl.program_id(0)

        def both(update):
            for place, query_ref in enumerate((own_ref, recv_ref)):
                for head, query in enumerate(masked_queries(query_ref[...])):
                    update(head, pl.ds(place * rows, rows), query)

        @pl.when(step == 0)
        def _():
            def start(head, at, query):
                total = weigh(query, text_key_ref[...], text_value_ref[...])
                if extra:
                    total += weigh(query, fresh_refs[0][...], with_ones(fresh_refs[1][...]))
                acc_ref[head, at] = total

            both(start)

        value_block = with_ones(value_ref[0])

        def more(head, at, query):
            acc_ref[head, at] += weigh(query, key_ref[0], value_block)

        both(more)

    whole = lambda shape: pl.BlockSpec(shape, lambda i, od: (0,) * len(shape))
    block = pl.BlockSpec((1, patch_rows, LANES), lambda i, od: (od[i], 0, 0))
    total_keys = blocks * patch_rows + TEXT_PAD + (patch_rows if extra else 0)
    return pl.pallas_call(
        kernel,
        out_shape=jax.ShapeDtypeStruct((2, 2 * rows, 2 * LANES), F32),
        grid_spec=pltpu.PrefetchScalarGridSpec(
            num_scalar_prefetch=1,
            grid=(blocks,),
            in_specs=[whole((rows, LANES)), whole((rows, LANES)), block, block]
            + [whole(text_keys.shape), whole(text_values.shape)]
            + [whole(array.shape) for array in fresh],
            out_specs=whole((2, 2 * rows, 2 * LANES)),
        ),
        compiler_params=params(),
        cost_estimate=cost(
            4 * 2 * rows * 2 * total_keys * 256, 4 * LANES * total_keys, 4 * rows * total_keys
        ),
        name="attend_stale",
    )(order, own, recv, keys, values, text_keys, text_values, *fresh)


def attend_fresh(place, owns, recvs, accs, chunk):
    count = len(owns)
    sizes = [array.shape[0] for array in owns]
    total = 2 * sum(sizes)
    hops = [k for group in GROUPS for k in group]
    steps = len(hops)

    def kernel(place_ref, *refs):
        own_refs, recv_refs, acc_refs = refs[:count], refs[count : 2 * count], refs[2 * count : 3 * count]
        out_ref, keys_ref, values_ref = refs[3 * count :]
        at = 0
        for own_ref, recv_ref, size in zip(own_refs, recv_refs, sizes):
            for ref in (own_ref, recv_ref):
                keys_ref[at : at + size] = ref[:, LANES : 2 * LANES]
                values_ref[at : at + size] = ref[:, 2 * LANES :]
                at += size
        value_block = with_ones(values_ref[...])
        hop_at = 0
        for own_ref, recv_ref, acc_ref, size in zip(own_refs, recv_refs, acc_refs, sizes):
            for side, ref in enumerate((own_ref, recv_ref)):
                sums = []
                for head, query in enumerate(masked_queries(ref[:, 0:LANES])):
                    sums.append(
                        acc_ref[head, side * size : (side + 1) * size]
                        + weigh(query, keys_ref[...], value_block)
                    )
                lane = lax.broadcasted_iota(jnp.int32, (size, LANES), 1)
                top = jnp.where(lane < HEAD, sums[0][:, :LANES], sums[1][:, :LANES])
                bottom = jnp.where(lane < HEAD, sums[0][:, LANES:], sums[1][:, LANES:])
                result = top / bottom
                for index in range(size // chunk):
                    target = lax.rem(place_ref[0] + steps - hops[hop_at + index], steps)
                    out_ref[target, side] = result[index * chunk : (index + 1) * chunk].astype(BF)
            hop_at += size // chunk

    vmem = pl.BlockSpec(memory_space=pltpu.VMEM)
    return pl.pallas_call(
        kernel,
        out_shape=[
            jax.ShapeDtypeStruct((steps, 2, chunk, LANES), BF),
            jax.ShapeDtypeStruct((total, LANES), BF),
            jax.ShapeDtypeStruct((total, LANES), BF),
        ],
        in_specs=[pl.BlockSpec(memory_space=pltpu.SMEM)] + [vmem] * (3 * count),
        out_specs=[vmem] * 3,
        compiler_params=params(),
        cost_estimate=cost(4 * total * 2 * total * 256, 8 * total * 1024, 2 * total * total),
        name="attend_fresh",
    )(place, *owns, *recvs, *accs)


def out_project(attended, weight):
    sources, _, chunk, _ = attended.shape
    width = weight.shape[1]
    pair = 2

    def kernel(attended_ref, weight_ref, own_ref, other_ref):
        step = pl.program_id(0)
        parts = [
            jnp.concatenate([attended_ref[at, side] for at in range(pair)], axis=1)
            for side in range(2)
        ]
        sums = [jnp.dot(part, weight_ref[...], preferred_element_type=F32) for part in parts]

        @pl.when(step == 0)
        def _():
            own_ref[...] = sums[0]
            other_ref[...] = sums[1]

        @pl.when(step > 0)
        def _():
            own_ref[...] += sums[0]
            other_ref[...] += sums[1]

    return pl.pallas_call(
        kernel,
        out_shape=[jax.ShapeDtypeStruct((chunk, width), F32)] * 2,
        grid=(sources // pair,),
        in_specs=[
            pl.BlockSpec((pair, 2, chunk, LANES), lambda i: (i, 0, 0, 0)),
            pl.BlockSpec((pair * LANES, width), lambda i: (i, 0)),
        ],
        out_specs=[pl.BlockSpec((chunk, width), lambda i: (0, 0))] * 2,
        compiler_params=params(),
        cost_estimate=cost(4 * chunk * sources * LANES * width, 2 * weight.size),
        name="out_project",
    )(attended, weight)


def finish(level, hidden, own, recv, mod_table, final_mod, final_weight):
    rows, width = hidden.shape
    channels = final_weight.shape[1]

    def kernel(level_ref, hidden_ref, own_ref, recv_ref, mod_ref, final_ref, weight_ref, out_ref, vel_ref):
        projected = own_ref[...] + recv_ref[...].astype(F32)
        updated = hidden_ref[...].astype(F32) + mod_ref[0, 2:3] * projected
        out_ref[...] = updated
        values = normalize(updated)
        normed = (values * (1.0 + final_ref[0, 1:2]) + final_ref[0, 0:1]).astype(BF)
        vel_ref[...] = jnp.dot(normed, weight_ref[...], preferred_element_type=F32)

    whole = lambda shape: pl.BlockSpec(shape, lambda i, lv: (0,) * len(shape))
    return pl.pallas_call(
        kernel,
        out_shape=[
            jax.ShapeDtypeStruct((rows, width), F32),
            jax.ShapeDtypeStruct((rows, channels), F32),
        ],
        grid_spec=pltpu.PrefetchScalarGridSpec(
            num_scalar_prefetch=1,
            grid=(1,),
            in_specs=[
                whole((rows, width)),
                whole((rows, width)),
                whole((rows, width)),
                pl.BlockSpec((1, 3, width), lambda i, lv: (lv[0], 0, 0)),
                pl.BlockSpec((1, 2, width), lambda i, lv: (lv[0], 0, 0)),
                whole((width, channels)),
            ],
            out_specs=[whole((rows, width)), whole((rows, channels))],
        ),
        compiler_params=params(),
        cost_estimate=cost(20 * rows * width, 16 * rows * width),
        name="finish",
    )(level, hidden, own, recv, mod_table, final_mod, final_weight)


def embed(patch, flags, scales, velocity, partner, latent, updated, weight, positions):
    rows, width = updated.shape
    channels = latent.shape[1]

    def kernel(patch_ref, flag_ref, scale_ref, vel_ref, partner_ref, latent_ref, updated_ref, weight_ref, pos_ref, out_ref, new_ref):
        first = flag_ref[0] == 0
        last = flag_ref[1] == 1
        velocity, partner = vel_ref[...], partner_ref[...]
        conditional = jnp.where(first, velocity, partner)
        unconditional = jnp.where(first, partner, velocity)
        guided = unconditional + scale_ref[0] * (conditional - unconditional)
        latent = latent_ref[...]
        moved = latent + scale_ref[1] * guided
        new_ref[...] = jnp.where(last, moved, latent)
        embedded = jnp.dot(moved.astype(BF), weight_ref[...], preferred_element_type=F32)
        embedded = embedded + pos_ref[0].astype(F32)
        out_ref[...] = jnp.where(last, embedded, updated_ref[...]).astype(BF)

    whole = lambda shape: pl.BlockSpec(shape, lambda i, pt: (0,) * len(shape))
    smem = pl.BlockSpec(memory_space=pltpu.SMEM)
    return pl.pallas_call(
        kernel,
        out_shape=[
            jax.ShapeDtypeStruct((rows, width), BF),
            jax.ShapeDtypeStruct((rows, channels), F32),
        ],
        grid_spec=pltpu.PrefetchScalarGridSpec(
            num_scalar_prefetch=1,
            grid=(1,),
            in_specs=[
                smem,
                smem,
                whole((rows, channels)),
                whole((rows, channels)),
                whole((rows, channels)),
                whole((rows, width)),
                whole((channels, width)),
                pl.BlockSpec((1, rows, width), lambda i, pt: (pt[0], 0, 0)),
            ],
            out_specs=[whole((rows, width)), whole((rows, channels))],
        ),
        compiler_params=params(),
        cost_estimate=cost(2 * rows * width * channels, 10 * rows * width),
        name="embed",
    )(patch, flags, scales, velocity, partner, latent, updated, weight, positions)


def on_device(
    hidden_in,
    latent_in,
    kv_cache,
    text_kv,
    qkv_weight,
    out_weight,
    mod_table,
    final_mod,
    final_weight,
    embed_weight,
    pos_embed,
    patch_order,
    step_index,
    guidance,
):
    sections = lax.axis_size("section")
    members = lax.axis_size("patch")
    ring = members // 2
    section = lax.axis_index("section")
    branch = lax.axis_index("cfg")
    place = lax.axis_index("patch") // 2

    def along_z(value, hops):
        pairs = [(at, (at + 2 * hops) % members) for at in range(members)]
        return lax.ppermute(value, "patch", pairs)

    def across_x(value):
        return lax.ppermute(value, "patch", [(at, at ^ 1) for at in range(members)])

    def across_cfg(value):
        return lax.ppermute(value, "cfg", [(0, 1), (1, 0)])

    def next_section(value):
        return lax.ppermute(value, "section", [(at, (at + 1) % sections) for at in range(sections)])

    columns = [[2 * z + x for z in range(ring)] for x in range(2)]
    hidden = hidden_in[0, 0]
    latent = latent_in[0]
    chunk = hidden.shape[0]
    patch_rows = chunk * members
    modulation = mod_table[0]
    depth = qkv_weight.shape[1]

    weight_flat = qkv_weight[0].reshape(depth, 3 * LANES)
    weight_both = jnp.concatenate([weight_flat, across_x(weight_flat)], axis=1)
    out_all = lax.all_gather(
        out_weight[0], "patch", axis=0, tiled=True, axis_index_groups=columns
    )
    cache = kv_cache[0, 0]
    keys = cache[:, 0].reshape(-1, patch_rows, LANES)
    values = cache[:, 1].reshape(-1, patch_rows, LANES)
    text = text_kv[0, 0]
    pad = ((0, TEXT_PAD - text.shape[0]), (0, 0))
    text_keys = jnp.pad(text[:, 0], pad)
    text_values = jnp.pad(
        jnp.concatenate([text[:, 1], jnp.ones((text.shape[0], LANES), BF)], axis=1), pad
    )
    guide_scale = guidance[0].astype(F32) / 64.0
    is_last = section == sections - 1
    rolled = jnp.take(patch_order, (jnp.arange(sections) + sections - 1 - section) % sections)
    flags = jnp.stack([branch, is_last.astype(jnp.int32)]).astype(jnp.int32)
    fresh = ()
    for tick in range(TICKS):
        position = sections - 1 + tick - section
        offset = (position >= sections).astype(jnp.int32)
        level = step_index + offset
        normed = norm_rows(hidden, modulation, level)
        owns, recvs, accs = [], [], []
        for group in GROUPS:
            chunks = [along_z(normed, hops) if hops else normed for hops in group]
            own, other = project(chunks, weight_both)
            owns.append(own)
            recvs.append(across_x(other))
        stale = rolled[1 + tick :]
        for own, recv in zip(owns, recvs):
            accs.append(attend_stale(stale, own, recv, keys, values, text_keys, text_values, fresh))
        attended, *fresh = attend_fresh(place[None].astype(jnp.int32), owns, recvs, accs, chunk)
        attended = lax.all_to_all(
            attended, "patch", 0, 0, axis_index_groups=columns
        )
        mine, theirs = out_project(attended, out_all)
        updated, velocity = finish(
            level, hidden, mine, across_x(theirs.astype(BF)), modulation, final_mod, final_weight
        )
        scales = jnp.stack([guide_scale, (sigma_of(level + 1) - sigma_of(level))[0]])
        outgoing, latent = embed(
            rolled[tick][None],
            flags,
            scales,
            velocity,
            across_cfg(velocity),
            latent,
            updated,
            embed_weight,
            pos_embed,
        )
        hidden, latent = next_section(outgoing), next_section(latent)
    return (hidden.astype(F32)[None, None], latent[None])


def solution(mesh):
    placed = (
        P("cfg", "section", "patch", None),
        P("section", "patch", None),
        P("cfg", "section", None, None, "patch"),
        P("cfg", "section", None, None, "patch"),
        P("section", None, None, "patch"),
        P("section", "patch", None),
        P("section", None, None, None),
        P(),
        P(),
        P(),
        P(None, "patch", None),
        P(),
        P(),
        P(),
    )
    return jax.shard_map(
        on_device,
        mesh=mesh,
        in_specs=placed,
        out_specs=(P("cfg", "section", "patch", None), P("section", "patch", None)),
        check_vma=False,
    )
```

```python
import math

import jax
import jax.numpy as jnp
from jax import lax
from jax.experimental import pallas as pl
from jax.experimental.pallas import tpu as pltpu
from jax.sharding import PartitionSpec as P

HEAD = 64
NT = 28
TICKS = 2
EPSILON = 1e-06
BF = jnp.bfloat16
F32 = jnp.float32
VMEM_LIMIT = 20 * 1024 * 1024
Q_SCALE = math.log2(math.e) / math.sqrt(HEAD)
GROUPS = ((0, 1, -1, 2), (-2, 3, -3, 4))
SPLIT = 24
LANES = 128
TEXT_PAD = 384


def params():
    return pltpu.CompilerParams(vmem_limit_bytes=VMEM_LIMIT)


def cost(flops, moved, exps=0):
    return pl.CostEstimate(flops=int(flops), bytes_accessed=int(moved), transcendentals=int(exps))


def sigma_of(time_level):
    frac = 1.0 - time_level.astype(F32) / NT
    return 3.0 * frac / (1.0 + 2.0 * frac)


def normalize(values):
    center = values - jnp.mean(values, axis=-1, keepdims=True)
    return center / jnp.sqrt(jnp.mean(center * center, axis=-1, keepdims=True) + EPSILON)


def on_whole(kernel, outs, args, scalars, estimate, name, scratch=(), tokens=()):
    vmem = pl.BlockSpec(memory_space=pltpu.VMEM)
    used, waited = len(args), len(tokens)

    def body(*refs):
        kernel(*refs[:used], *refs[used + waited :])

    return pl.pallas_call(
        body,
        out_shape=[jax.ShapeDtypeStruct(shape, dtype) for shape, dtype in outs],
        in_specs=[pl.BlockSpec(memory_space=pltpu.SMEM)] * scalars
        + [vmem] * (used - scalars)
        + [pl.BlockSpec(memory_space=pl.ANY)] * waited,
        out_specs=[vmem] * len(outs),
        scratch_shapes=list(scratch),
        compiler_params=params(),
        cost_estimate=estimate,
        name=name,
    )(*args, *tokens)


def after(value, *tokens):
    anywhere = pl.BlockSpec(memory_space=pl.ANY)
    return pl.pallas_call(
        lambda *refs: None,
        out_shape=jax.ShapeDtypeStruct(value.shape, value.dtype),
        in_specs=[anywhere] * (1 + len(tokens)),
        out_specs=anywhere,
        input_output_aliases={0: 0},
        compiler_params=params(),
        cost_estimate=cost(0, 0),
        name="after",
    )(value, *tokens)


def cut(left, right, rows_left, rows_right, token):
    width = left.shape[1]

    def kernel(left_ref, right_ref, *outs):
        for ref, rows, out in zip((left_ref, right_ref), (rows_left, rows_right), outs):
            out[...] = ref[rows[0] : rows[1]]

    return on_whole(
        kernel,
        [((rows[1] - rows[0], width), BF) for rows in (rows_left, rows_right)],
        [left, right],
        0,
        cost(0, 400 * width),
        "cut",
        tokens=[token],
    )


def on_whole(kernel, outs, args, scalars, estimate, name, scratch=(), tokens=()):
    vmem = pl.BlockSpec(memory_space=pltpu.VMEM)
    used, waited = len(args), len(tokens)

    def body(*refs):
        kernel(*refs[:used], *refs[used + waited :])

    return pl.pallas_call(
        body,
        out_shape=[jax.ShapeDtypeStruct(shape, dtype) for shape, dtype in outs],
        in_specs=[pl.BlockSpec(memory_space=pltpu.SMEM)] * scalars
        + [vmem] * (used - scalars)
        + [pl.BlockSpec(memory_space=pl.ANY)] * waited,
        out_specs=[vmem] * len(outs),
        scratch_shapes=list(scratch),
        compiler_params=params(),
        cost_estimate=estimate,
        name=name,
    )(*args, *tokens)


def after(value, *tokens):
    anywhere = pl.BlockSpec(memory_space=pl.ANY)
    return pl.pallas_call(
        lambda *refs: None,
        out_shape=jax.ShapeDtypeStruct(value.shape, value.dtype),
        in_specs=[anywhere] * (1 + len(tokens)),
        out_specs=anywhere,
        input_output_aliases={0: 0},
        compiler_params=params(),
        cost_estimate=cost(0, 0),
        name="after",
    )(value, *tokens)


def cut(left, right, rows_left, rows_right, token):
    width = left.shape[1]

    def kernel(left_ref, right_ref, *outs):
        for ref, rows, out in zip((left_ref, right_ref), (rows_left, rows_right), outs):
            out[...] = ref[rows[0] : rows[1]]

    return on_whole(
        kernel,
        [((rows[1] - rows[0], width), BF) for rows in (rows_left, rows_right)],
        [left, right],
        0,
        cost(0, 400 * width),
        "cut",
        tokens=[token],
    )


def pick(table, wanted):
    return lax.dynamic_index_in_dim(table, wanted, 0, keepdims=False)


def modulate(hidden, shift, scale):
    return (normalize(hidden) * (1.0 + scale) + shift).astype(BF)


def norm_first(info, hidden, mod_table):
    rows, width = hidden.shape
    vmem = pl.BlockSpec(memory_space=pltpu.VMEM)

    def kernel(info_ref, hidden_ref, mod_ref, out_ref):
        out_ref[...] = modulate(hidden_ref[...], mod_ref[0, 0:1], mod_ref[0, 1:2])

    return pl.pallas_call(
        kernel,
        out_shape=jax.ShapeDtypeStruct((rows, width), BF),
        grid_spec=pltpu.PrefetchScalarGridSpec(
            num_scalar_prefetch=1,
            grid=(1,),
            in_specs=[vmem, pl.BlockSpec((1, 3, width), lambda i, nf: (nf[3], 0, 0))],
            out_specs=vmem,
        ),
        compiler_params=params(),
        cost_estimate=cost(10 * rows * width, 6 * rows * width),
        name="norm_first",
    )(info, hidden, mod_table)


def norm_rows(hidden, mods):
    rows, width = hidden.shape[0], mods.shape[1]

    def kernel(hidden_ref, mod_ref, out_ref):
        values = hidden_ref[:, :width].astype(F32)
        out_ref[...] = modulate(values, mod_ref[0:1], mod_ref[1:2])

    return on_whole(
        kernel,
        [((rows, width), BF)],
        [hidden, mods],
        0,
        cost(10 * rows * width, 6 * rows * width),
        "norm_rows",
    )[0]


def prepare(info, order, mod_table, final_mod, pos_embed):
    width = mod_table.shape[2]
    chunk = pos_embed.shape[1]

    def kernel(info_ref, order_ref, *refs):
        for source, target in zip(refs[: 3 * TICKS], refs[3 * TICKS :]):
            target[...] = source[0]

    def spec(rows, index):
        return pl.BlockSpec((1, rows, width), lambda i, nf, od: (index(nf, od), 0, 0))

    specs, operands, outs = [], [], []
    for tick in range(TICKS):
        for table, index in (
            (mod_table, lambda nf, od, tick=tick: nf[3 + tick]),
            (final_mod, lambda nf, od, tick=tick: nf[3 + tick]),
            (pos_embed, lambda nf, od, tick=tick: od[tick]),
        ):
            specs.append(spec(table.shape[1], index))
            operands.append(table)
            outs.append(jax.ShapeDtypeStruct(table.shape[1:], table.dtype))
    found = pl.pallas_call(
        kernel,
        out_shape=outs,
        grid_spec=pltpu.PrefetchScalarGridSpec(
            num_scalar_prefetch=2,
            grid=(1,),
            in_specs=specs,
            out_specs=[pl.BlockSpec(memory_space=pltpu.VMEM)] * len(outs),
        ),
        compiler_params=params(),
        cost_estimate=cost(0, 8 * chunk * width),
        name="prepare",
    )(info, order, *operands)
    return found[0::3], found[1::3], found[2::3]


def join_halves(info, near, far, width):
    reach = near.shape[1]

    def kernel(info_ref, near_ref, far_ref, out_ref):
        first = info_ref[1] == 0
        near, far = near_ref[...], far_ref[...]
        out_ref[:, :reach] = jnp.where(first, near, far)
        out_ref[:, reach:] = jnp.where(first, far, near)[:, 2 * reach - width :]

    return on_whole(
        kernel,
        [((3, width, LANES), BF)],
        [info, near, far],
        1,
        cost(0, 6 * width * LANES),
        "join_halves",
    )[0]


def head_scale(values, factor):
    lane = lax.broadcasted_iota(jnp.int32, values.shape, 1)
    square = values * values
    low = jnp.sum(jnp.where(lane < HEAD, square, 0.0), axis=1, keepdims=True)
    high = jnp.sum(jnp.where(lane < HEAD, 0.0, square), axis=1, keepdims=True)
    total = jnp.where(lane < HEAD, low, high)
    return values * (factor / jnp.sqrt(total * (1.0 / HEAD) + EPSILON))


def project(pieces, weight, tokens=()):
    count = len(pieces)
    width = pieces[0].shape[1]
    rows = [piece.shape[0] for piece in pieces]
    total = sum(rows)

    def kernel(*refs):
        piece_refs, (weight_ref, out_ref, gathered) = refs[:count], refs[count:]
        for at, ref in enumerate(piece_refs):
            start = sum(rows[:at])
            gathered[start : start + rows[at], :] = ref[...].astype(F32)
        mixed = jnp.dot(
            gathered[...].astype(BF),
            jnp.concatenate([weight_ref[at] for at in range(3)], axis=1),
            preferred_element_type=F32,
        )
        out_ref[:, 0:LANES] = head_scale(mixed[:, 0:LANES], Q_SCALE).astype(BF)
        out_ref[:, LANES : 2 * LANES] = head_scale(mixed[:, LANES : 2 * LANES], 1.0).astype(BF)
        out_ref[:, 2 * LANES :] = mixed[:, 2 * LANES :].astype(BF)

    return on_whole(
        kernel,
        [((total, 3 * LANES), BF)],
        [*pieces, weight],
        0,
        cost(2 * total * width * 3 * LANES, 6 * LANES * width + 2 * total * width),
        "project",
        [pltpu.VMEM((total, width), F32)],
        tokens,
    )[0]


def masked_queries(queries):
    lane = lax.broadcasted_iota(jnp.int32, queries.shape, 1)
    zero = jnp.zeros_like(queries)
    return jnp.where(lane < HEAD, queries, zero), jnp.where(lane < HEAD, zero, queries)


def weigh(query, keys, values):
    scores = lax.dot_general(
        query, keys, (((1,), (1,)), ((), ())), preferred_element_type=F32
    )
    return jnp.dot(jnp.exp2(scores).astype(BF), values, preferred_element_type=F32)


def with_ones(values):
    return jnp.concatenate([values, jnp.ones(values.shape, BF)], axis=1)


def attend_stale(tick, info, order, mixed, cache, text_keys, text_values, fresh):
    rows = mixed.shape[0]
    patches, patch_rows = cache.shape[1:3]
    blocks = patches - 1 - tick
    extra = len(fresh)

    def kernel(info_ref, order_ref, mixed_ref, cache_ref, text_key_ref, text_value_ref, *rest):
        fresh_refs, acc_ref = rest[:extra], rest[extra]
        places = [
            order_ref[lax.rem(2 * patches + tick - info_ref[2] + block, patches)]
            for block in range(blocks)
        ]
        queries = masked_queries(mixed_ref[:, 0:LANES])
        loads = [lambda: (text_key_ref[...], text_value_ref[...])]
        if extra:
            loads.append(lambda: (fresh_refs[0][...], with_ones(fresh_refs[1][...])))
        for at in places:
            loads.append(lambda at=at: (cache_ref[0, at], with_ones(cache_ref[1, at])))
        totals = [0.0, 0.0]
        for at in range(0, len(loads), 2):
            sets = [load() for load in loads[at : at + 2]]
            key_set = jnp.concatenate([each[0] for each in sets], axis=0)
            value_set = jnp.concatenate([each[1] for each in sets], axis=0)
            for head, query in enumerate(queries):
                totals[head] = totals[head] + weigh(query, key_set, value_set)
        for head, total in enumerate(totals):
            acc_ref[head * rows : (head + 1) * rows] = total

    total_keys = blocks * patch_rows + TEXT_PAD + (patch_rows if extra else 0)
    vmem = pl.BlockSpec(memory_space=pltpu.VMEM)
    smem = pl.BlockSpec(memory_space=pltpu.SMEM)
    return pl.pallas_call(
        kernel,
        out_shape=jax.ShapeDtypeStruct((2 * rows, 2 * LANES), F32),
        in_specs=[smem, smem] + [vmem] * (4 + extra),
        out_specs=vmem,
        compiler_params=params(),
        cost_estimate=cost(
            4 * 2 * rows * total_keys * 256, 4 * LANES * total_keys, 2 * rows * total_keys
        ),
        name="attend_stale",
    )(info, order, mixed, cache, text_keys, text_values, *fresh)


def attend_fresh(place, mixed, accs, chunk):
    count = len(mixed)
    sizes = [array.shape[0] for array in mixed]
    total = sum(sizes)
    hops = [k for group in GROUPS for k in group]
    steps = len(hops)

    def kernel(place_ref, *refs):
        mixed_refs, acc_refs = refs[:count], refs[count : 2 * count]
        out_ref, keys_ref, values_ref = refs[2 * count :]
        at = 0
        for ref, size in zip(mixed_refs, sizes):
            keys_ref[at : at + size] = ref[:, LANES : 2 * LANES]
            values_ref[at : at + size] = ref[:, 2 * LANES :]
            at += size
        value_block = with_ones(values_ref[...])
        hop_at = 0
        for at, (ref, acc_ref, size) in enumerate(zip(mixed_refs, acc_refs, sizes)):
            sums = [
                acc_ref[head * size : (head + 1) * size] + weigh(query, keys_ref[...], value_block)
                for head, query in enumerate(masked_queries(ref[:, 0:LANES]))
            ]
            lane = lax.broadcasted_iota(jnp.int32, (size, LANES), 1)
            top = jnp.where(lane < HEAD, sums[0][:, :LANES], sums[1][:, :LANES])
            bottom = jnp.where(lane < HEAD, sums[0][:, LANES:], sums[1][:, LANES:])
            result = top / bottom
            result = jnp.where(place_ref[1] == 0, result, pltpu.roll(result, HEAD, 1))
            for index in range(size // chunk):
                target = lax.rem(place_ref[0] + steps - hops[hop_at + index], steps)
                out_ref[target, at % 2] = result[index * chunk : (index + 1) * chunk].astype(BF)
            if at % 2:
                hop_at += size // chunk

    vmem = pl.BlockSpec(memory_space=pltpu.VMEM)
    return pl.pallas_call(
        kernel,
        out_shape=[
            jax.ShapeDtypeStruct((steps, 2, chunk, LANES), BF),
            jax.ShapeDtypeStruct((total, LANES), BF),
            jax.ShapeDtypeStruct((total, LANES), BF),
        ],
        in_specs=[pl.BlockSpec(memory_space=pltpu.SMEM)] + [vmem] * (2 * count),
        out_specs=[vmem] * 3,
        compiler_params=params(),
        cost_estimate=cost(4 * total * 2 * total * 256, 8 * total * 1024, 2 * total * total),
        name="attend_fresh",
    )(place, *mixed, *accs)


def out_project(attended, first, second, hidden, mods):
    sources, _, chunk, _ = attended.shape
    width = first.shape[1]

    def kernel(attended_ref, first_ref, second_ref, hidden_ref, mod_ref, sum_ref, flip_ref):
        lane = lax.broadcasted_iota(jnp.int32, (2 * chunk, LANES), 1)
        gate = mod_ref[2:3]
        blocks = [
            jnp.concatenate([attended_ref[at, side].astype(F32) for side in range(2)], axis=0)
            for at in range(sources)
        ]
        lefts, rights = [], []
        for even, odd in zip(blocks[::2], blocks[1::2]):
            lefts.append(jnp.where(lane < HEAD, even, pltpu.roll(odd, HEAD, 1)).astype(BF))
            rights.append(jnp.where(lane < HEAD, pltpu.roll(even, HEAD, 1), odd).astype(BF))
        sums = jnp.dot(
            jnp.concatenate(lefts, axis=1), first_ref[...], preferred_element_type=F32
        ) + jnp.dot(jnp.concatenate(rights, axis=1), second_ref[...], preferred_element_type=F32)
        sum_ref[...] = hidden_ref[:, :width].astype(F32) + gate * sums[:chunk]
        flip_ref[...] = (gate * sums[chunk:]).astype(BF)

    return on_whole(
        kernel,
        [((chunk, width), F32), ((chunk, width), BF)],
        [attended, first, second, hidden, mods],
        0,
        cost(4 * chunk * sources * LANES * width, 4 * first.size),
        "out_project",
    )


def finish(partial, recv, final_mods, final_weight):
    rows, width = partial.shape
    channels = final_weight.shape[0]

    def kernel(partial_ref, recv_ref, final_ref, weight_ref, vel_ref, out_ref):
        updated = partial_ref[...] + recv_ref[...].astype(F32)
        out_ref[...] = updated.astype(BF)
        normed = modulate(updated, final_ref[0:1], final_ref[1:2])
        vel_ref[...] = lax.dot_general(
            normed, weight_ref[...], (((1,), (1,)), ((), ())), preferred_element_type=F32
        )

    return on_whole(
        kernel,
        [((rows, channels), F32), ((rows, width), BF)],
        [partial, recv, final_mods, final_weight],
        0,
        cost(20 * rows * width, 16 * rows * width),
        "finish",
    )


def embed(tick, info, guidance, velocity, partner, latent, weight, positions, updated):
    rows, width = positions.shape
    start = latent.shape[1] - 2 * LANES

    def kernel(info_ref, guide_ref, vel_ref, partner_ref, latent_ref, weight_ref, pos_ref, updated_ref, out_ref):
        first = info_ref[1] == 0
        last = info_ref[5] == 1
        level = jnp.full((rows, LANES), info_ref[3 + tick], jnp.int32)
        guide = jnp.full((rows, LANES), guide_ref[0], jnp.int32).astype(F32) / 64.0
        velocity, partner = vel_ref[...], partner_ref[...]
        conditional = jnp.where(first, velocity, partner)
        unconditional = jnp.where(first, partner, velocity)
        guided = unconditional + guide * (conditional - unconditional)
        latent = latent_ref[:, start : start + LANES].astype(F32)
        latent = latent + latent_ref[:, start + LANES :].astype(F32)
        moved = latent + (sigma_of(level + 1) - sigma_of(level)) * guided
        embedded = jnp.dot(moved.astype(BF), weight_ref[...], preferred_element_type=F32)
        embedded = (embedded + pos_ref[...].astype(F32)).astype(BF)
        out_ref[:, :width] = jnp.where(last, embedded, updated_ref[...])
        latent = jnp.where(last, moved, latent)
        high = latent.astype(BF)
        out_ref[:, width : width + LANES] = high
        out_ref[:, width + LANES :] = (latent - high.astype(F32)).astype(BF)

    return on_whole(
        kernel,
        [((rows, width + 2 * LANES), BF)],
        [info, guidance, velocity, partner, latent, weight, positions, updated],
        2,
        cost(2 * rows * width * LANES, 10 * rows * width),
        "embed",
    )[0]


def on_device(
    hidden_in,
    latent_in,
    kv_cache,
    text_kv,
    qkv_weight,
    out_weight,
    mod_table,
    final_mod,
    final_weight,
    embed_weight,
    pos_embed,
    patch_order,
    step_index,
    guidance,
):
    sections = lax.axis_size("section")
    members = lax.axis_size("patch")
    ring = members // 2
    section = lax.axis_index("section")
    branch = lax.axis_index("cfg")
    place = lax.axis_index("patch") // 2

    def along_z(value, hops):
        pairs = [(at, (at + 2 * hops) % members) for at in range(members)]
        return lax.ppermute(value, "patch", pairs)

    def across_x(value):
        return lax.ppermute(value, "patch", [(at, at ^ 1) for at in range(members)])

    def across_cfg(value):
        return lax.ppermute(value, "cfg", [(0, 1), (1, 0)])

    def between(value, moves, flip):
        pairs = [
            (source * members + at, target * members + (at ^ flip))
            for source, target in moves
            for at in range(members)
        ]
        return lax.ppermute(value, ("section", "patch"), pairs)

    last = sections - 1
    around = [(at, (at + 1) % sections) for at in range(sections)]
    columns = [[2 * z + x for z in range(ring)] for x in range(2)]
    chunk, width = hidden_in.shape[2:]
    channels = latent_in.shape[2]
    spare = ((0, 0), (0, LANES - channels))
    latent = jnp.pad(latent_in[0], ((0, 0), (0, 2 * LANES - channels)))
    weight_final = jnp.pad(jnp.transpose(final_weight), (spare[1], spare[0]))
    weight_embed = jnp.pad(embed_weight, (spare[1], spare[0]))
    patch_rows = chunk * members
    depth = qkv_weight.shape[1]

    info = jnp.stack(
        [
            place,
            branch,
            section,
            step_index[0] + (last - section >= sections).astype(jnp.int32),
            step_index[0] + (last + 1 - section >= sections).astype(jnp.int32),
            (section == last).astype(jnp.int32),
        ]
    ).astype(jnp.int32)
    out_half = lax.dynamic_slice_in_dim(out_weight[0], branch * HEAD, HEAD, 0)
    out_first = lax.all_gather(
        out_half, "patch", axis=0, tiled=True, axis_index_groups=columns
    )
    hidden = hidden_in[0, 0]
    normed = norm_first(info, hidden, mod_table[0])
    fresh = ()
    for tick in range(TICKS):
        if tick:
            hidden = arrived
            normed = norm_rows(hidden, mods[tick])
        got = {0: normed, 1: along_z(normed, 1), -1: along_z(normed, -1)}
        if tick == 0:
            weight_own = jnp.transpose(qkv_weight[0], (1, 0, 2))
            reach = (depth // 2 + LANES - 1) // LANES * LANES
            half = jnp.where(branch == 0, weight_own[:, :reach], weight_own[:, depth - reach :])
            mods, final_mods, positions = prepare(
                info, patch_order, mod_table[0], final_mod, pos_embed
            )
            got[1] = after(got[1], half, mods[0])
            near = across_x(half)
            cache = jnp.transpose(kv_cache[0, 0], (1, 0, 2)).reshape(2, -1, patch_rows, LANES)
            text = text_kv[0, 0]
            pad = ((0, TEXT_PAD - text.shape[0]), (0, 0))
            text_keys = jnp.pad(text[:, 0], pad)
            text_values = jnp.pad(
                jnp.concatenate([text[:, 1], jnp.ones((text.shape[0], LANES), BF)], axis=1), pad
            )
        got[2], got[-2] = along_z(got[1], 1), along_z(got[-1], -1)
        if tick == 0:
            near = after(near, got[2], got[-2])
            got[2] = after(got[2], cache, text_keys, text_values)
            weight_other = join_halves(info, near, across_cfg(near), depth)
        got[3], got[-3] = along_z(got[2], 1), along_z(got[-2], -1)
        mixed, accs = [], []

        def attend_group(pieces, tokens):
            other = across_x(project(pieces, weight_other, tokens))
            for part in (project(pieces, weight_own), other):
                mixed.append(part)
                accs.append(
                    attend_stale(
                        tick, info, patch_order, part, cache, text_keys, text_values, fresh
                    )
                )

        attend_group([got[hops] for hops in GROUPS[0]], ())
        ahead, behind = cut(got[3], got[-3], (0, SPLIT), (SPLIT, chunk), accs[0])
        got[4] = [along_z(ahead, 1), along_z(behind, -1)]
        attend_group([got[hops] for hops in GROUPS[1][:-1]] + got[4], (accs[1],))
        if tick == 0:
            out_first = after(out_first, accs[2])
            out_second = across_cfg(out_first)
        attended, *fresh = attend_fresh(info, mixed, accs, chunk)
        attended = lax.all_to_all(attended, "patch", 0, 0, axis_index_groups=columns)
        partial, flip = out_project(attended, out_first, out_second, hidden, mods[tick])
        velocity, updated = finish(partial, across_x(flip), final_mods[tick], weight_final)
        outgoing = embed(
            tick,
            info,
            guidance,
            velocity,
            across_cfg(velocity),
            arrived if tick else latent,
            weight_embed,
            positions[tick],
            updated,
        )
        arrived = between(outgoing, around, 0)
    hidden_out = arrived[:, :width].astype(F32)
    latent_out = arrived[:, width : width + channels].astype(F32) + arrived[
        :, width + LANES : width + LANES + channels
    ].astype(F32)
    return (hidden_out[None, None], latent_out[None])


def solution(mesh):
    placed = (
        P("cfg", "section", "patch", None),
        P("section", "patch", None),
        P("cfg", "section", None, None, "patch"),
        P("cfg", "section", None, None, "patch"),
        P("section", None, None, "patch"),
        P("section", "patch", None),
        P("section", None, None, None),
        P(),
        P(),
        P(),
        P(None, "patch", None),
        P(),
        P(),
        P(),
    )
    return jax.shard_map(
        on_device,
        mesh=mesh,
        in_specs=placed,
        out_specs=(P("cfg", "section", "patch", None), P("section", "patch", None)),
        check_vma=False,
    )
```

```python
import math

import jax
import jax.numpy as jnp
from jax import lax
from jax.experimental import pallas as pl
from jax.experimental.pallas import tpu as pltpu
from jax.sharding import PartitionSpec as P

HEAD = 64
NT = 28
TICKS = 2
EPSILON = 1e-06
BF = jnp.bfloat16
F32 = jnp.float32
VMEM_LIMIT = 20 * 1024 * 1024
Q_SCALE = math.log2(math.e) / math.sqrt(HEAD)
GROUPS = ((0, 1, -1, 2), (-2, 3, -3, 4))
SPLIT = 24
HOPS = (0, 1, 2, 3, -3, -2, -1, 4)
LANES = 128
TEXT_PAD = 384


def params():
    return pltpu.CompilerParams(vmem_limit_bytes=VMEM_LIMIT)


def cost(flops, moved, exps=0):
    return pl.CostEstimate(flops=int(flops), bytes_accessed=int(moved), transcendentals=int(exps))


def sigma_of(time_level):
    frac = 1.0 - time_level.astype(F32) / NT
    return 3.0 * frac / (1.0 + 2.0 * frac)


def normalize(values):
    center = values - jnp.mean(values, axis=-1, keepdims=True)
    return center / jnp.sqrt(jnp.mean(center * center, axis=-1, keepdims=True) + EPSILON)


def on_whole(kernel, outs, args, scalars, estimate, name, scratch=(), tokens=()):
    vmem = pl.BlockSpec(memory_space=pltpu.VMEM)
    used, waited = len(args), len(tokens)

    def body(*refs):
        kernel(*refs[:used], *refs[used + waited :])

    return pl.pallas_call(
        body,
        out_shape=[jax.ShapeDtypeStruct(shape, dtype) for shape, dtype in outs],
        in_specs=[pl.BlockSpec(memory_space=pltpu.SMEM)] * scalars
        + [vmem] * (used - scalars)
        + [pl.BlockSpec(memory_space=pl.ANY)] * waited,
        out_specs=[vmem] * len(outs),
        scratch_shapes=list(scratch),
        compiler_params=params(),
        cost_estimate=estimate,
        name=name,
    )(*args, *tokens)


def after(value, *tokens):
    anywhere = pl.BlockSpec(memory_space=pl.ANY)
    return pl.pallas_call(
        lambda *refs: None,
        out_shape=jax.ShapeDtypeStruct(value.shape, value.dtype),
        in_specs=[anywhere] * (1 + len(tokens)),
        out_specs=anywhere,
        input_output_aliases={0: 0},
        compiler_params=params(),
        cost_estimate=cost(0, 0),
        name="after",
    )(value, *tokens)


def cut(left, right, rows_left, rows_right, tokens):
    width = left.shape[1]

    def kernel(left_ref, right_ref, *outs):
        for ref, rows, out in zip((left_ref, right_ref), (rows_left, rows_right), outs):
            out[...] = ref[rows[0] : rows[1]]

    return on_whole(
        kernel,
        [((rows[1] - rows[0], width), BF) for rows in (rows_left, rows_right)],
        [left, right],
        0,
        cost(0, 400 * width),
        "cut",
        tokens=tokens,
    )


def modulate(hidden, shift, scale):
    return (normalize(hidden) * (1.0 + scale) + shift).astype(BF)


def norm_first(info, hidden, mod_table, out_weight):
    rows, width = hidden.shape
    vmem = pl.BlockSpec(memory_space=pltpu.VMEM)

    def kernel(info_ref, hidden_ref, mod_ref, weight_ref, out_ref):
        out_ref[:HEAD] = jnp.where(info_ref[1] == 0, weight_ref[:HEAD], weight_ref[HEAD:])
        out_ref[HEAD:] = modulate(hidden_ref[...], mod_ref[0, 0:1], mod_ref[0, 1:2])

    return pl.pallas_call(
        kernel,
        out_shape=jax.ShapeDtypeStruct((HEAD + rows, width), BF),
        grid_spec=pltpu.PrefetchScalarGridSpec(
            num_scalar_prefetch=1,
            grid=(1,),
            in_specs=[vmem, pl.BlockSpec((1, 3, width), lambda i, nf: (nf[3], 0, 0)), vmem],
            out_specs=vmem,
        ),
        compiler_params=params(),
        cost_estimate=cost(10 * rows * width, 6 * rows * width),
        name="norm_first",
    )(info, hidden, mod_table, out_weight)


def select_half(info, weight, reach, token):
    planes, width, lanes = weight.shape

    def kernel(info_ref, weight_ref, out_ref):
        out_ref[...] = jnp.where(
            info_ref[1] == 0, weight_ref[:, :reach], weight_ref[:, width - reach :]
        )

    return on_whole(
        kernel,
        [((planes, reach, lanes), BF)],
        [info, weight],
        1,
        cost(0, 8 * planes * reach * lanes),
        "select_half",
        tokens=[token],
    )[0]


def stack_weights(pieces, token):
    count = len(pieces)
    width = pieces[0].shape[1]

    def kernel(*refs):
        for at, ref in enumerate(refs[:-1]):
            refs[-1][at * HEAD : (at + 1) * HEAD] = ref[:HEAD]

    return on_whole(
        kernel,
        [((count * HEAD, width), BF)],
        pieces,
        0,
        cost(0, 4 * count * HEAD * width),
        "stack_weights",
        tokens=[token],
    )[0]


def norm_rows(hidden, mods):
    rows, width = hidden.shape[0], mods.shape[1]

    def kernel(hidden_ref, mod_ref, out_ref):
        values = hidden_ref[:, :width].astype(F32)
        out_ref[...] = modulate(values, mod_ref[0:1], mod_ref[1:2])

    return on_whole(
        kernel,
        [((rows, width), BF)],
        [hidden, mods],
        0,
        cost(10 * rows * width, 6 * rows * width),
        "norm_rows",
    )[0]


def prepare(info, order, mod_table, final_mod, pos_embed):
    width = mod_table.shape[2]
    chunk = pos_embed.shape[1]

    def kernel(info_ref, order_ref, *refs):
        for source, target in zip(refs[: 3 * TICKS], refs[3 * TICKS :]):
            target[...] = source[0]

    def spec(rows, index):
        return pl.BlockSpec((1, rows, width), lambda i, nf, od: (index(nf, od), 0, 0))

    specs, operands, outs = [], [], []
    for tick in range(TICKS):
        for table, index in (
            (mod_table, lambda nf, od, tick=tick: nf[3 + tick]),
            (final_mod, lambda nf, od, tick=tick: nf[3 + tick]),
            (pos_embed, lambda nf, od, tick=tick: od[tick]),
        ):
            specs.append(spec(table.shape[1], index))
            operands.append(table)
            outs.append(jax.ShapeDtypeStruct(table.shape[1:], table.dtype))
    found = pl.pallas_call(
        kernel,
        out_shape=outs,
        grid_spec=pltpu.PrefetchScalarGridSpec(
            num_scalar_prefetch=2,
            grid=(1,),
            in_specs=specs,
            out_specs=[pl.BlockSpec(memory_space=pltpu.VMEM)] * len(outs),
        ),
        compiler_params=params(),
        cost_estimate=cost(0, 8 * chunk * width),
        name="prepare",
    )(info, order, *operands)
    return found[0::3], found[1::3], found[2::3]


def join_halves(info, near, far, width):
    reach = near.shape[1]

    def kernel(info_ref, near_ref, far_ref, out_ref):
        first = info_ref[1] == 0
        near, far = near_ref[...], far_ref[...]
        out_ref[:, :reach] = jnp.where(first, near, far)
        out_ref[:, reach:] = jnp.where(first, far, near)[:, 2 * reach - width :]

    return on_whole(
        kernel,
        [((3, width, LANES), BF)],
        [info, near, far],
        1,
        cost(0, 6 * width * LANES),
        "join_halves",
    )[0]


def head_scale(values, factor):
    lane = lax.broadcasted_iota(jnp.int32, values.shape, 1)
    square = values * values
    low = jnp.sum(jnp.where(lane < HEAD, square, 0.0), axis=1, keepdims=True)
    high = jnp.sum(jnp.where(lane < HEAD, 0.0, square), axis=1, keepdims=True)
    total = jnp.where(lane < HEAD, low, high)
    return values * (factor / jnp.sqrt(total * (1.0 / HEAD) + EPSILON))


def project(pieces, weight, tokens=()):
    count = len(pieces)
    width = pieces[0].shape[1]
    rows = [piece.shape[0] - HEAD * (piece.shape[0] > HEAD) for piece in pieces]
    total = sum(rows)

    def kernel(*refs):
        piece_refs, (weight_ref, out_ref, gathered) = refs[:count], refs[count:]
        for at, ref in enumerate(piece_refs):
            start = sum(rows[:at])
            gathered[start : start + rows[at], :] = ref[ref.shape[0] - rows[at] :].astype(F32)
        mixed = jnp.dot(
            gathered[...].astype(BF),
            jnp.concatenate([weight_ref[at] for at in range(3)], axis=1),
            preferred_element_type=F32,
        )
        out_ref[:, 0:LANES] = head_scale(mixed[:, 0:LANES], Q_SCALE).astype(BF)
        out_ref[:, LANES : 2 * LANES] = head_scale(mixed[:, LANES : 2 * LANES], 1.0).astype(BF)
        out_ref[:, 2 * LANES :] = mixed[:, 2 * LANES :].astype(BF)

    return on_whole(
        kernel,
        [((total, 3 * LANES), BF)],
        [*pieces, weight],
        0,
        cost(2 * total * width * 3 * LANES, 6 * LANES * width + 2 * total * width),
        "project",
        [pltpu.VMEM((total, width), F32)],
        tokens,
    )[0]


def masked_queries(queries):
    lane = lax.broadcasted_iota(jnp.int32, queries.shape, 1)
    zero = jnp.zeros_like(queries)
    return jnp.where(lane < HEAD, queries, zero), jnp.where(lane < HEAD, zero, queries)


def weigh(query, keys, values):
    scores = lax.dot_general(
        query, keys, (((1,), (1,)), ((), ())), preferred_element_type=F32
    )
    return jnp.dot(jnp.exp2(scores).astype(BF), values, preferred_element_type=F32)


def with_ones(values):
    return jnp.concatenate([values, jnp.ones(values.shape, BF)], axis=1)


def attend_stale(tick, info, order, mixed, cache, text_keys, text_values, fresh):
    rows = mixed.shape[0]
    patches, patch_rows = cache.shape[1:3]
    blocks = patches - 1 - tick
    extra = len(fresh)

    def kernel(info_ref, order_ref, mixed_ref, cache_ref, text_key_ref, text_value_ref, *rest):
        fresh_refs, acc_ref = rest[:extra], rest[extra]
        places = [
            order_ref[lax.rem(2 * patches + tick - info_ref[2] + block, patches)]
            for block in range(blocks)
        ]
        queries = masked_queries(mixed_ref[:, 0:LANES])
        loads = [lambda: (text_key_ref[...], text_value_ref[...])]
        if extra:
            loads.append(lambda: (fresh_refs[0][...], with_ones(fresh_refs[1][...])))
        for at in places:
            loads.append(lambda at=at: (cache_ref[0, at], with_ones(cache_ref[1, at])))
        totals = [0.0, 0.0]
        for at in range(0, len(loads), 2):
            sets = [load() for load in loads[at : at + 2]]
            key_set = jnp.concatenate([each[0] for each in sets], axis=0)
            value_set = jnp.concatenate([each[1] for each in sets], axis=0)
            for head, query in enumerate(queries):
                totals[head] = totals[head] + weigh(query, key_set, value_set)
        for head, total in enumerate(totals):
            acc_ref[head * rows : (head + 1) * rows] = total

    total_keys = blocks * patch_rows + TEXT_PAD + (patch_rows if extra else 0)
    vmem = pl.BlockSpec(memory_space=pltpu.VMEM)
    smem = pl.BlockSpec(memory_space=pltpu.SMEM)
    return pl.pallas_call(
        kernel,
        out_shape=jax.ShapeDtypeStruct((2 * rows, 2 * LANES), F32),
        in_specs=[smem, smem] + [vmem] * (4 + extra),
        out_specs=vmem,
        compiler_params=params(),
        cost_estimate=cost(
            4 * 2 * rows * total_keys * 256, 4 * LANES * total_keys, 2 * rows * total_keys
        ),
        name="attend_stale",
    )(info, order, mixed, cache, text_keys, text_values, *fresh)


def attend_fresh(place, mixed, accs, chunk):
    count = len(mixed)
    sizes = [array.shape[0] for array in mixed]
    total = sum(sizes)
    hops = [k for group in GROUPS for k in group]
    steps = len(hops)

    def kernel(place_ref, *refs):
        mixed_refs, acc_refs = refs[:count], refs[count : 2 * count]
        out_ref, keys_ref, values_ref = refs[2 * count :]
        at = 0
        for ref, size in zip(mixed_refs, sizes):
            keys_ref[at : at + size] = ref[:, LANES : 2 * LANES]
            values_ref[at : at + size] = ref[:, 2 * LANES :]
            at += size
        value_block = with_ones(values_ref[...])
        hop_at = 0
        for at, (ref, acc_ref, size) in enumerate(zip(mixed_refs, acc_refs, sizes)):
            sums = [
                acc_ref[head * size : (head + 1) * size] + weigh(query, keys_ref[...], value_block)
                for head, query in enumerate(masked_queries(ref[:, 0:LANES]))
            ]
            lane = lax.broadcasted_iota(jnp.int32, (size, LANES), 1)
            top = jnp.where(lane < HEAD, sums[0][:, :LANES], sums[1][:, :LANES])
            bottom = jnp.where(lane < HEAD, sums[0][:, LANES:], sums[1][:, LANES:])
            result = top / bottom
            result = jnp.where(place_ref[1] == 0, result, pltpu.roll(result, HEAD, 1))
            for index in range(size // chunk):
                target = lax.rem(place_ref[0] + steps - hops[hop_at + index], steps)
                out_ref[target, at % 2] = result[index * chunk : (index + 1) * chunk].astype(BF)
            if at % 2:
                hop_at += size // chunk

    vmem = pl.BlockSpec(memory_space=pltpu.VMEM)
    return pl.pallas_call(
        kernel,
        out_shape=[
            jax.ShapeDtypeStruct((steps, 2, chunk, LANES), BF),
            jax.ShapeDtypeStruct((total, LANES), BF),
            jax.ShapeDtypeStruct((total, LANES), BF),
        ],
        in_specs=[pl.BlockSpec(memory_space=pltpu.SMEM)] + [vmem] * (2 * count),
        out_specs=[vmem] * 3,
        compiler_params=params(),
        cost_estimate=cost(4 * total * 2 * total * 256, 8 * total * 1024, 2 * total * total),
        name="attend_fresh",
    )(place, *mixed, *accs)


def out_project(info, attended, weights, hidden, mods):
    sources, _, chunk, _ = attended.shape
    width = mods.shape[1]

    def kernel(info_ref, attended_ref, *refs):
        weight_refs, (hidden_ref, mod_ref, sum_ref, flip_ref) = refs[:4], refs[4:]
        lane = lax.broadcasted_iota(jnp.int32, (2 * chunk, LANES), 1)
        gate = mod_ref[2:3]
        blocks = []
        for hop in HOPS:
            at = lax.rem(info_ref[0] + sources - hop, sources)
            blocks.append(
                jnp.concatenate([attended_ref[at, side].astype(F32) for side in range(2)], axis=0)
            )
        halves = ([], [])
        for even, odd in zip(blocks[::2], blocks[1::2]):
            halves[0].append(jnp.where(lane < HEAD, even, pltpu.roll(odd, HEAD, 1)).astype(BF))
            halves[1].append(jnp.where(lane < HEAD, pltpu.roll(even, HEAD, 1), odd).astype(BF))
        sums = 0.0
        for half, (main_ref, final_ref) in zip(halves, (weight_refs[:2], weight_refs[2:])):
            whole = main_ref.shape[0] // LANES
            tail = jnp.concatenate([main_ref[whole * LANES :], final_ref[...]], axis=0)
            sums = sums + jnp.dot(
                jnp.concatenate(half[:whole], axis=1),
                main_ref[: whole * LANES],
                preferred_element_type=F32,
            )
            sums = sums + jnp.dot(half[whole], tail, preferred_element_type=F32)
        sum_ref[...] = hidden_ref[:, :width].astype(F32) + gate * sums[:chunk]
        flip_ref[...] = (gate * sums[chunk:]).astype(BF)

    return on_whole(
        kernel,
        [((chunk, width), F32), ((chunk, width), BF)],
        [info, attended, *weights, hidden, mods],
        1,
        cost(4 * chunk * sources * LANES * width, 4 * sources * HEAD * width),
        "out_project",
    )


def finish(partial, recv, final_mods, final_weight):
    rows, width = partial.shape
    channels = final_weight.shape[0]

    def kernel(partial_ref, recv_ref, final_ref, weight_ref, vel_ref, out_ref):
        updated = partial_ref[...] + recv_ref[...].astype(F32)
        out_ref[...] = updated.astype(BF)
        normed = modulate(updated, final_ref[0:1], final_ref[1:2])
        vel_ref[...] = lax.dot_general(
            normed, weight_ref[...], (((1,), (1,)), ((), ())), preferred_element_type=F32
        )

    return on_whole(
        kernel,
        [((rows, channels), F32), ((rows, width), BF)],
        [partial, recv, final_mods, final_weight],
        0,
        cost(20 * rows * width, 16 * rows * width),
        "finish",
    )


def embed(tick, info, guidance, velocity, partner, latent, weight, positions, updated):
    rows, width = positions.shape
    start = latent.shape[1] - 2 * LANES

    def kernel(info_ref, guide_ref, vel_ref, partner_ref, latent_ref, weight_ref, pos_ref, updated_ref, out_ref):
        first = info_ref[1] == 0
        last = info_ref[5] == 1
        level = jnp.full((rows, LANES), info_ref[3 + tick], jnp.int32)
        guide = jnp.full((rows, LANES), guide_ref[0], jnp.int32).astype(F32) / 64.0
        velocity, partner = vel_ref[...], partner_ref[...]
        conditional = jnp.where(first, velocity, partner)
        unconditional = jnp.where(first, partner, velocity)
        guided = unconditional + guide * (conditional - unconditional)
        latent = latent_ref[:, start : start + LANES].astype(F32)
        latent = latent + latent_ref[:, start + LANES :].astype(F32)
        moved = latent + (sigma_of(level + 1) - sigma_of(level)) * guided
        embedded = jnp.dot(moved.astype(BF), weight_ref[...], preferred_element_type=F32)
        embedded = (embedded + pos_ref[...].astype(F32)).astype(BF)
        out_ref[:, :width] = jnp.where(last, embedded, updated_ref[...])
        latent = jnp.where(last, moved, latent)
        high = latent.astype(BF)
        out_ref[:, width : width + LANES] = high
        out_ref[:, width + LANES :] = (latent - high.astype(F32)).astype(BF)

    return on_whole(
        kernel,
        [((rows, width + 2 * LANES), BF)],
        [info, guidance, velocity, partner, latent, weight, positions, updated],
        2,
        cost(2 * rows * width * LANES, 10 * rows * width),
        "embed",
    )[0]


def on_device(
    hidden_in,
    latent_in,
    kv_cache,
    text_kv,
    qkv_weight,
    out_weight,
    mod_table,
    final_mod,
    final_weight,
    embed_weight,
    pos_embed,
    patch_order,
    step_index,
    guidance,
):
    sections = lax.axis_size("section")
    members = lax.axis_size("patch")
    ring = members // 2
    section = lax.axis_index("section")
    branch = lax.axis_index("cfg")
    place = lax.axis_index("patch") // 2

    def along_z(value, hops):
        pairs = [(at, (at + 2 * hops) % members) for at in range(members)]
        return lax.ppermute(value, "patch", pairs)

    def across_x(value):
        return lax.ppermute(value, "patch", [(at, at ^ 1) for at in range(members)])

    def across_cfg(value):
        return lax.ppermute(value, "cfg", [(0, 1), (1, 0)])

    def between(value, moves, flip):
        pairs = [
            (source * members + at, target * members + (at ^ flip))
            for source, target in moves
            for at in range(members)
        ]
        return lax.ppermute(value, ("section", "patch"), pairs)

    last = sections - 1
    around = [(at, (at + 1) % sections) for at in range(sections)]
    columns = [[2 * z + x for z in range(ring)] for x in range(2)]
    chunk, width = hidden_in.shape[2:]
    channels = latent_in.shape[2]
    spare = ((0, 0), (0, LANES - channels))
    latent = jnp.pad(latent_in[0], ((0, 0), (0, 2 * LANES - channels)))
    weight_final = jnp.pad(jnp.transpose(final_weight), (spare[1], spare[0]))
    weight_embed = jnp.pad(embed_weight, (spare[1], spare[0]))
    patch_rows = chunk * members
    depth = qkv_weight.shape[1]

    info = jnp.stack(
        [
            place,
            branch,
            section,
            step_index[0] + (last - section >= sections).astype(jnp.int32),
            step_index[0] + (last + 1 - section >= sections).astype(jnp.int32),
            (section == last).astype(jnp.int32),
        ]
    ).astype(jnp.int32)
    hidden = hidden_in[0, 0]
    normed = norm_first(info, hidden, mod_table[0], out_weight[0])
    fresh = ()
    for tick in range(TICKS):
        if tick:
            hidden = arrived
            normed = norm_rows(hidden, mods[tick])
        got = {0: normed, 1: along_z(normed, 1), -1: along_z(normed, -1)}
        if tick == 0:
            weight_own = jnp.transpose(qkv_weight[0], (1, 0, 2))
            reach = (depth // 2 + LANES - 1) // LANES * LANES
            half = select_half(info, weight_own, reach, normed)
            mods, final_mods, positions = prepare(
                info, patch_order, mod_table[0], final_mod, pos_embed
            )
            got[1] = after(got[1], half, mods[0])
            near = across_x(half)
            cache = jnp.transpose(kv_cache[0, 0], (1, 0, 2)).reshape(2, -1, patch_rows, LANES)
            text = text_kv[0, 0]
            pad = ((0, TEXT_PAD - text.shape[0]), (0, 0))
            text_keys = jnp.pad(text[:, 0], pad)
            text_values = jnp.pad(
                jnp.concatenate([text[:, 1], jnp.ones((text.shape[0], LANES), BF)], axis=1), pad
            )
        got[2], got[-2] = along_z(got[1], 1), along_z(got[-1], -1)
        if tick == 0:
            near = after(near, got[2], got[-2])
            got[2] = after(got[2], cache, text_keys, text_values)
            weight_other = join_halves(info, near, across_cfg(near), depth)
        got[3], got[-3] = along_z(got[2], 1), along_z(got[-2], -1)
        mixed, accs, others = [], [], []

        def attend_group(pieces, tokens):
            others.append(project(pieces, weight_other, tokens))
            for part in (project(pieces, weight_own), across_x(others[-1])):
                mixed.append(part)
                accs.append(
                    attend_stale(
                        tick, info, patch_order, part, cache, text_keys, text_values, fresh
                    )
                )

        attend_group([got[hops] for hops in GROUPS[0]], ())
        if tick == 0:
            rows, weight = cut(got[3], got[-3], (HEAD, HEAD + chunk), (0, HEAD), [accs[0], others[0]])
            got[4] = [along_z(rows, 1)]
            final = along_z(weight, -1)
            main = stack_weights([got[hops] for hops in HOPS[:-1]], weight)
            out_weights = (main, final, across_cfg(main), across_cfg(final))
            waited = (accs[1], main)
        else:
            ahead, behind = cut(got[3], got[-3], (0, SPLIT), (SPLIT, chunk), [accs[0], others[0]])
            got[4] = [along_z(ahead, 1), along_z(behind, -1)]
            waited = (accs[1],)
        attend_group([got[hops] for hops in GROUPS[1][:-1]] + got[4], waited)
        attended, *fresh = attend_fresh(info, mixed, accs, chunk)
        attended = lax.all_to_all(attended, "patch", 0, 0, axis_index_groups=columns)
        partial, flip = out_project(info, attended, out_weights, hidden, mods[tick])
        velocity, updated = finish(partial, across_x(flip), final_mods[tick], weight_final)
        outgoing = embed(
            tick,
            info,
            guidance,
            velocity,
            across_cfg(velocity),
            arrived if tick else latent,
            weight_embed,
            positions[tick],
            updated,
        )
        arrived = between(outgoing, around, 0)
    hidden_out = arrived[:, :width].astype(F32)
    latent_out = arrived[:, width : width + channels].astype(F32) + arrived[
        :, width + LANES : width + LANES + channels
    ].astype(F32)
    return (hidden_out[None, None], latent_out[None])


def solution(mesh):
    placed = (
        P("cfg", "section", "patch", None),
        P("section", "patch", None),
        P("cfg", "section", None, None, "patch"),
        P("cfg", "section", None, None, "patch"),
        P("section", None, None, "patch"),
        P("section", "patch", None),
        P("section", None, None, None),
        P(),
        P(),
        P(),
        P(None, "patch", None),
        P(),
        P(),
        P(),
    )
    return jax.shard_map(
        on_device,
        mesh=mesh,
        in_specs=placed,
        out_specs=(P("cfg", "section", "patch", None), P("section", "patch", None)),
        check_vma=False,
    )
```

```python
import math

import jax
import jax.numpy as jnp
from jax import lax
from jax.experimental import pallas as pl
from jax.experimental.pallas import tpu as pltpu
from jax.sharding import PartitionSpec as P

HEAD = 64
NT = 28
TICKS = 2
EPSILON = 1e-06
BF = jnp.bfloat16
F32 = jnp.float32
VMEM_LIMIT = 20 * 1024 * 1024
Q_SCALE = math.log2(math.e) / math.sqrt(HEAD)
GROUPS = ((0, 1, -1, 2), (-2, 3, -3, 4))
SPLIT = 24
HOPS = (0, 1, 2, 3, -3, -2, -1, 4)
LANES = 128
TEXT_PAD = 384


def params():
    return pltpu.CompilerParams(vmem_limit_bytes=VMEM_LIMIT)


def cost(flops, moved, exps=0):
    return pl.CostEstimate(flops=int(flops), bytes_accessed=int(moved), transcendentals=int(exps))


def sigma_of(time_level):
    frac = 1.0 - time_level.astype(F32) / NT
    return 3.0 * frac / (1.0 + 2.0 * frac)


def normalize(values):
    center = values - jnp.mean(values, axis=-1, keepdims=True)
    return center / jnp.sqrt(jnp.mean(center * center, axis=-1, keepdims=True) + EPSILON)


def on_whole(kernel, outs, args, scalars, estimate, name, scratch=(), tokens=()):
    vmem = pl.BlockSpec(memory_space=pltpu.VMEM)
    used, waited = len(args), len(tokens)

    def body(*refs):
        kernel(*refs[:used], *refs[used + waited :])

    return pl.pallas_call(
        body,
        out_shape=[jax.ShapeDtypeStruct(shape, dtype) for shape, dtype in outs],
        in_specs=[pl.BlockSpec(memory_space=pltpu.SMEM)] * scalars
        + [vmem] * (used - scalars)
        + [pl.BlockSpec(memory_space=pl.ANY)] * waited,
        out_specs=[vmem] * len(outs),
        scratch_shapes=list(scratch),
        compiler_params=params(),
        cost_estimate=estimate,
        name=name,
    )(*args, *tokens)


def after(value, *tokens):
    anywhere = pl.BlockSpec(memory_space=pl.ANY)
    return pl.pallas_call(
        lambda *refs: None,
        out_shape=jax.ShapeDtypeStruct(value.shape, value.dtype),
        in_specs=[anywhere] * (1 + len(tokens)),
        out_specs=anywhere,
        input_output_aliases={0: 0},
        compiler_params=params(),
        cost_estimate=cost(0, 0),
        name="after",
    )(value, *tokens)


def cut(left, right, rows_left, rows_right, tokens):
    width = left.shape[1]

    def kernel(left_ref, right_ref, *outs):
        for ref, rows, out in zip((left_ref, right_ref), (rows_left, rows_right), outs):
            out[...] = ref[rows[0] : rows[1]]

    return on_whole(
        kernel,
        [((rows[1] - rows[0], width), BF) for rows in (rows_left, rows_right)],
        [left, right],
        0,
        cost(0, 400 * width),
        "cut",
        tokens=tokens,
    )


def modulate(hidden, shift, scale):
    return (normalize(hidden) * (1.0 + scale) + shift).astype(BF)


def norm_first(info, hidden, mod_table, out_weight):
    rows, width = hidden.shape
    vmem = pl.BlockSpec(memory_space=pltpu.VMEM)

    def kernel(info_ref, hidden_ref, mod_ref, weight_ref, out_ref):
        out_ref[:HEAD] = jnp.where(info_ref[1] == 0, weight_ref[:HEAD], weight_ref[HEAD:])
        out_ref[HEAD:] = modulate(hidden_ref[...], mod_ref[0, 0:1], mod_ref[0, 1:2])

    return pl.pallas_call(
        kernel,
        out_shape=jax.ShapeDtypeStruct((HEAD + rows, width), BF),
        grid_spec=pltpu.PrefetchScalarGridSpec(
            num_scalar_prefetch=1,
            grid=(1,),
            in_specs=[vmem, pl.BlockSpec((1, 3, width), lambda i, nf: (nf[3], 0, 0)), vmem],
            out_specs=vmem,
        ),
        compiler_params=params(),
        cost_estimate=cost(10 * rows * width, 6 * rows * width),
        name="norm_first",
    )(info, hidden, mod_table, out_weight)


def select_half(info, weight, reach, token):
    planes, width, lanes = weight.shape

    def kernel(info_ref, weight_ref, out_ref):
        out_ref[...] = jnp.where(
            info_ref[1] == 0, weight_ref[:, :reach], weight_ref[:, width - reach :]
        )

    return on_whole(
        kernel,
        [((planes, reach, lanes), BF)],
        [info, weight],
        1,
        cost(0, 8 * planes * reach * lanes),
        "select_half",
        tokens=[token],
    )[0]


def stack_weights(pieces, token):
    count = len(pieces)
    width = pieces[0].shape[1]

    def kernel(*refs):
        for at, ref in enumerate(refs[:-1]):
            refs[-1][at * HEAD : (at + 1) * HEAD] = ref[:HEAD]

    return on_whole(
        kernel,
        [((count * HEAD, width), BF)],
        pieces,
        0,
        cost(0, 4 * count * HEAD * width),
        "stack_weights",
        tokens=[token],
    )[0]


def norm_rows(hidden, mods):
    rows, width = hidden.shape[0], mods.shape[1]

    def kernel(hidden_ref, mod_ref, out_ref):
        values = hidden_ref[:, :width].astype(F32)
        out_ref[...] = modulate(values, mod_ref[0:1], mod_ref[1:2])

    return on_whole(
        kernel,
        [((rows, width), BF)],
        [hidden, mods],
        0,
        cost(10 * rows * width, 6 * rows * width),
        "norm_rows",
    )[0]


def prepare(info, order, mod_table, final_mod, pos_embed):
    width = mod_table.shape[2]
    chunk = pos_embed.shape[1]

    def kernel(info_ref, order_ref, *refs):
        for source, target in zip(refs[: 3 * TICKS], refs[3 * TICKS :]):
            target[...] = source[0]

    def spec(rows, index):
        return pl.BlockSpec((1, rows, width), lambda i, nf, od: (index(nf, od), 0, 0))

    specs, operands, outs = [], [], []
    for tick in range(TICKS):
        for table, index in (
            (mod_table, lambda nf, od, tick=tick: nf[3 + tick]),
            (final_mod, lambda nf, od, tick=tick: nf[3 + tick]),
            (pos_embed, lambda nf, od, tick=tick: od[tick]),
        ):
            specs.append(spec(table.shape[1], index))
            operands.append(table)
            outs.append(jax.ShapeDtypeStruct(table.shape[1:], table.dtype))
    found = pl.pallas_call(
        kernel,
        out_shape=outs,
        grid_spec=pltpu.PrefetchScalarGridSpec(
            num_scalar_prefetch=2,
            grid=(1,),
            in_specs=specs,
            out_specs=[pl.BlockSpec(memory_space=pltpu.VMEM)] * len(outs),
        ),
        compiler_params=params(),
        cost_estimate=cost(0, 8 * chunk * width),
        name="prepare",
    )(info, order, *operands)
    return found[0::3], found[1::3], found[2::3]


def join_halves(info, near, far, width):
    reach = near.shape[1]

    def kernel(info_ref, near_ref, far_ref, out_ref):
        first = info_ref[1] == 0
        near, far = near_ref[...], far_ref[...]
        out_ref[:, :reach] = jnp.where(first, near, far)
        out_ref[:, reach:] = jnp.where(first, far, near)[:, 2 * reach - width :]

    return on_whole(
        kernel,
        [((3, width, LANES), BF)],
        [info, near, far],
        1,
        cost(0, 6 * width * LANES),
        "join_halves",
    )[0]


def head_scale(values, factor):
    lane = lax.broadcasted_iota(jnp.int32, values.shape, 1)
    square = values * values
    low = jnp.sum(jnp.where(lane < HEAD, square, 0.0), axis=1, keepdims=True)
    high = jnp.sum(jnp.where(lane < HEAD, 0.0, square), axis=1, keepdims=True)
    total = jnp.where(lane < HEAD, low, high)
    return values * (factor / jnp.sqrt(total * (1.0 / HEAD) + EPSILON))


def project(pieces, weight, tokens=()):
    count = len(pieces)
    width = pieces[0].shape[1]
    rows = [piece.shape[0] - HEAD * (piece.shape[0] > HEAD) for piece in pieces]
    total = sum(rows)

    def kernel(*refs):
        piece_refs, (weight_ref, out_ref, gathered) = refs[:count], refs[count:]
        for at, ref in enumerate(piece_refs):
            start = sum(rows[:at])
            gathered[start : start + rows[at], :] = ref[ref.shape[0] - rows[at] :].astype(F32)
        mixed = jnp.dot(
            gathered[...].astype(BF),
            jnp.concatenate([weight_ref[at] for at in range(3)], axis=1),
            preferred_element_type=F32,
        )
        out_ref[:, 0:LANES] = head_scale(mixed[:, 0:LANES], Q_SCALE).astype(BF)
        out_ref[:, LANES : 2 * LANES] = head_scale(mixed[:, LANES : 2 * LANES], 1.0).astype(BF)
        out_ref[:, 2 * LANES :] = mixed[:, 2 * LANES :].astype(BF)

    return on_whole(
        kernel,
        [((total, 3 * LANES), BF)],
        [*pieces, weight],
        0,
        cost(2 * total * width * 3 * LANES, 6 * LANES * width + 2 * total * width),
        "project",
        [pltpu.VMEM((total, width), F32)],
        tokens,
    )[0]


def masked_queries(queries):
    lane = lax.broadcasted_iota(jnp.int32, queries.shape, 1)
    zero = jnp.zeros_like(queries)
    return jnp.where(lane < HEAD, queries, zero), jnp.where(lane < HEAD, zero, queries)


def weigh(query, keys, values):
    scores = lax.dot_general(
        query, keys, (((1,), (1,)), ((), ())), preferred_element_type=F32
    )
    return jnp.dot(jnp.exp2(scores).astype(BF), values, preferred_element_type=F32)


def with_ones(values):
    return jnp.concatenate([values, jnp.ones(values.shape, BF)], axis=1)


def attend_stale(tick, info, order, mixed, cache, text_keys, text_values, fresh):
    rows = mixed.shape[0]
    patches, patch_rows = cache.shape[1:3]
    blocks = patches - 1 - tick
    extra = len(fresh)

    def kernel(info_ref, order_ref, mixed_ref, cache_ref, text_key_ref, text_value_ref, *rest):
        fresh_refs, acc_ref = rest[:extra], rest[extra]
        places = [
            order_ref[lax.rem(2 * patches + tick - info_ref[2] + block, patches)]
            for block in range(blocks)
        ]
        queries = masked_queries(mixed_ref[:, 0:LANES])
        loads = [lambda: (text_key_ref[...], text_value_ref[...])]
        if extra:
            loads.append(lambda: (fresh_refs[0][...], with_ones(fresh_refs[1][...])))
        for at in places:
            loads.append(lambda at=at: (cache_ref[0, at], with_ones(cache_ref[1, at])))
        totals = [0.0, 0.0]
        for at in range(0, len(loads), 2):
            sets = [load() for load in loads[at : at + 2]]
            key_set = jnp.concatenate([each[0] for each in sets], axis=0)
            value_set = jnp.concatenate([each[1] for each in sets], axis=0)
            for head, query in enumerate(queries):
                totals[head] = totals[head] + weigh(query, key_set, value_set)
        for head, total in enumerate(totals):
            acc_ref[head * rows : (head + 1) * rows] = total

    total_keys = blocks * patch_rows + TEXT_PAD + (patch_rows if extra else 0)
    vmem = pl.BlockSpec(memory_space=pltpu.VMEM)
    smem = pl.BlockSpec(memory_space=pltpu.SMEM)
    return pl.pallas_call(
        kernel,
        out_shape=jax.ShapeDtypeStruct((2 * rows, 2 * LANES), F32),
        in_specs=[smem, smem] + [vmem] * (4 + extra),
        out_specs=vmem,
        compiler_params=params(),
        cost_estimate=cost(
            4 * 2 * rows * total_keys * 256, 4 * LANES * total_keys, 2 * rows * total_keys
        ),
        name="attend_stale",
    )(info, order, mixed, cache, text_keys, text_values, *fresh)


def attend_fresh(place, mixed, accs, chunk, keep):
    count = len(mixed)
    sizes = [array.shape[0] for array in mixed]
    total = sum(sizes)
    hops = [k for group in GROUPS for k in group]
    steps = len(hops)

    def kernel(place_ref, *refs):
        mixed_refs, acc_refs = refs[:count], refs[count : 2 * count]
        out_ref, keys_ref, values_ref = refs[2 * count :]
        at = 0
        for ref, size in zip(mixed_refs, sizes):
            keys_ref[at : at + size] = ref[:, LANES : 2 * LANES]
            values_ref[at : at + size] = ref[:, 2 * LANES :]
            at += size
        value_block = with_ones(values_ref[...])
        everyone = jnp.concatenate([ref[:, 0:LANES] for ref in mixed_refs], axis=0)
        sums = []
        for head, query in enumerate(masked_queries(everyone)):
            before = [
                acc_ref[head * size : (head + 1) * size] for acc_ref, size in zip(acc_refs, sizes)
            ]
            sums.append(
                jnp.concatenate(before, axis=0) + weigh(query, keys_ref[...], value_block)
            )
        lane = lax.broadcasted_iota(jnp.int32, (total, LANES), 1)
        top = jnp.where(lane < HEAD, sums[0][:, :LANES], sums[1][:, :LANES])
        bottom = jnp.where(lane < HEAD, sums[0][:, LANES:], sums[1][:, LANES:])
        result = top / bottom
        result = jnp.where(place_ref[1] == 0, result, pltpu.roll(result, HEAD, 1))
        row, hop_at = 0, 0
        for at, size in enumerate(sizes):
            for index in range(size // chunk):
                target = lax.rem(place_ref[0] + steps - hops[hop_at + index], steps)
                out_ref[target, at % 2] = result[row : row + chunk].astype(BF)
                row += chunk
            if at % 2:
                hop_at += size // chunk

    pair = [((total, LANES), BF)] * 2
    return on_whole(
        kernel,
        [((steps, 2, chunk, LANES), BF)] + (pair if keep else []),
        [place, *mixed, *accs],
        1,
        cost(4 * total * 2 * total * 256, 8 * total * 1024, 2 * total * total),
        "attend_fresh",
        [] if keep else [pltpu.VMEM(*each) for each in pair],
    )


def out_project(info, attended, weights, hidden, mods):
    sources, _, chunk, _ = attended.shape
    width = mods.shape[1]

    def kernel(info_ref, attended_ref, *refs):
        weight_refs, (hidden_ref, mod_ref, sum_ref, flip_ref) = refs[:4], refs[4:]
        lane = lax.broadcasted_iota(jnp.int32, (2 * chunk, LANES), 1)
        gate = mod_ref[2:3]
        blocks = []
        for hop in HOPS:
            at = lax.rem(info_ref[0] + sources - hop, sources)
            blocks.append(
                jnp.concatenate([attended_ref[at, side].astype(F32) for side in range(2)], axis=0)
            )
        halves = ([], [])
        for even, odd in zip(blocks[::2], blocks[1::2]):
            halves[0].append(jnp.where(lane < HEAD, even, pltpu.roll(odd, HEAD, 1)).astype(BF))
            halves[1].append(jnp.where(lane < HEAD, pltpu.roll(even, HEAD, 1), odd).astype(BF))
        sums = 0.0
        for half, (main_ref, final_ref) in zip(halves, (weight_refs[:2], weight_refs[2:])):
            whole = main_ref.shape[0] // LANES
            tail = jnp.concatenate([main_ref[whole * LANES :], final_ref[...]], axis=0)
            sums = sums + jnp.dot(
                jnp.concatenate(half[:whole], axis=1),
                main_ref[: whole * LANES],
                preferred_element_type=F32,
            )
            sums = sums + jnp.dot(half[whole], tail, preferred_element_type=F32)
        sum_ref[...] = hidden_ref[:, :width].astype(F32) + gate * sums[:chunk]
        flip_ref[...] = (gate * sums[chunk:]).astype(BF)

    return on_whole(
        kernel,
        [((chunk, width), F32), ((chunk, width), BF)],
        [info, attended, *weights, hidden, mods],
        1,
        cost(4 * chunk * sources * LANES * width, 4 * sources * HEAD * width),
        "out_project",
    )


def finish(partial, recv, final_mods, final_weight):
    rows, width = partial.shape
    channels = final_weight.shape[0]

    def kernel(partial_ref, recv_ref, final_ref, weight_ref, vel_ref, out_ref):
        updated = partial_ref[...] + recv_ref[...].astype(F32)
        out_ref[...] = updated.astype(BF)
        normed = modulate(updated, final_ref[0:1], final_ref[1:2])
        vel_ref[...] = lax.dot_general(
            normed, weight_ref[...], (((1,), (1,)), ((), ())), preferred_element_type=F32
        )

    return on_whole(
        kernel,
        [((rows, channels), F32), ((rows, width), BF)],
        [partial, recv, final_mods, final_weight],
        0,
        cost(20 * rows * width, 16 * rows * width),
        "finish",
    )


def embed(tick, info, guidance, velocity, partner, latent, weight, positions, updated):
    rows, width = positions.shape
    start = latent.shape[1] - 2 * LANES

    def kernel(info_ref, guide_ref, vel_ref, partner_ref, latent_ref, weight_ref, pos_ref, updated_ref, out_ref):
        first = info_ref[1] == 0
        last = info_ref[5] == 1
        level = jnp.full((rows, LANES), info_ref[3 + tick], jnp.int32)
        guide = jnp.full((rows, LANES), guide_ref[0], jnp.int32).astype(F32) / 64.0
        velocity, partner = vel_ref[...], partner_ref[...]
        conditional = jnp.where(first, velocity, partner)
        unconditional = jnp.where(first, partner, velocity)
        guided = unconditional + guide * (conditional - unconditional)
        latent = latent_ref[:, start : start + LANES].astype(F32)
        latent = latent + latent_ref[:, start + LANES :].astype(F32)
        moved = latent + (sigma_of(level + 1) - sigma_of(level)) * guided
        embedded = jnp.dot(moved.astype(BF), weight_ref[...], preferred_element_type=F32)
        embedded = (embedded + pos_ref[...].astype(F32)).astype(BF)
        out_ref[:, :width] = jnp.where(last, embedded, updated_ref[...])
        latent = jnp.where(last, moved, latent)
        high = latent.astype(BF)
        out_ref[:, width : width + LANES] = high
        out_ref[:, width + LANES :] = (latent - high.astype(F32)).astype(BF)

    return on_whole(
        kernel,
        [((rows, width + 2 * LANES), BF)],
        [info, guidance, velocity, partner, latent, weight, positions, updated],
        2,
        cost(2 * rows * width * LANES, 10 * rows * width),
        "embed",
    )[0]


def unpack(arrived, width, channels):
    rows = arrived.shape[0]

    def kernel(arrived_ref, hidden_ref, latent_ref):
        hidden_ref[...] = arrived_ref[:, :width].astype(F32)
        latent = arrived_ref[:, width : width + LANES].astype(F32)
        latent = latent + arrived_ref[:, width + LANES :].astype(F32)
        latent_ref[...] = latent[:, :channels]

    return on_whole(
        kernel,
        [((rows, width), F32), ((rows, channels), F32)],
        [arrived],
        0,
        cost(rows * width, 6 * rows * width),
        "unpack",
    )


def on_device(
    hidden_in,
    latent_in,
    kv_cache,
    text_kv,
    qkv_weight,
    out_weight,
    mod_table,
    final_mod,
    final_weight,
    embed_weight,
    pos_embed,
    patch_order,
    step_index,
    guidance,
):
    sections = lax.axis_size("section")
    members = lax.axis_size("patch")
    ring = members // 2
    section = lax.axis_index("section")
    branch = lax.axis_index("cfg")
    place = lax.axis_index("patch") // 2

    def along_z(value, hops):
        pairs = [(at, (at + 2 * hops) % members) for at in range(members)]
        return lax.ppermute(value, "patch", pairs)

    def across_x(value):
        return lax.ppermute(value, "patch", [(at, at ^ 1) for at in range(members)])

    def across_cfg(value):
        return lax.ppermute(value, "cfg", [(0, 1), (1, 0)])

    def between(value, moves, flip):
        pairs = [
            (source * members + at, target * members + (at ^ flip))
            for source, target in moves
            for at in range(members)
        ]
        return lax.ppermute(value, ("section", "patch"), pairs)

    last = sections - 1
    around = [(at, (at + 1) % sections) for at in range(sections)]
    columns = [[2 * z + x for z in range(ring)] for x in range(2)]
    chunk, width = hidden_in.shape[2:]
    channels = latent_in.shape[2]
    spare = ((0, 0), (0, LANES - channels))
    latent = jnp.pad(latent_in[0], ((0, 0), (0, 2 * LANES - channels)))
    weight_final = jnp.pad(jnp.transpose(final_weight), (spare[1], spare[0]))
    weight_embed = jnp.pad(embed_weight, (spare[1], spare[0]))
    patch_rows = chunk * members
    depth = qkv_weight.shape[1]

    info = jnp.stack(
        [
            place,
            branch,
            section,
            step_index[0] + (last - section >= sections).astype(jnp.int32),
            step_index[0] + (last + 1 - section >= sections).astype(jnp.int32),
            (section == last).astype(jnp.int32),
        ]
    ).astype(jnp.int32)
    hidden = hidden_in[0, 0]
    normed = norm_first(info, hidden, mod_table[0], out_weight[0])
    fresh = ()
    for tick in range(TICKS):
        if tick:
            hidden = arrived
            normed = norm_rows(hidden, mods[tick])
        got = {0: normed, 1: along_z(normed, 1), -1: along_z(normed, -1)}
        if tick == 0:
            weight_own = jnp.transpose(qkv_weight[0], (1, 0, 2))
            reach = (depth // 2 + LANES - 1) // LANES * LANES
            half = select_half(info, weight_own, reach, normed)
            mods, final_mods, positions = prepare(
                info, patch_order, mod_table[0], final_mod, pos_embed
            )
            got[1] = after(got[1], half, mods[0])
            near = across_x(half)
            cache = jnp.transpose(kv_cache[0, 0], (1, 0, 2)).reshape(2, -1, patch_rows, LANES)
            text = text_kv[0, 0]
            pad = ((0, TEXT_PAD - text.shape[0]), (0, 0))
            text_keys = jnp.pad(text[:, 0], pad)
            text_values = jnp.pad(
                jnp.concatenate([text[:, 1], jnp.ones((text.shape[0], LANES), BF)], axis=1), pad
            )
        got[2], got[-2] = along_z(got[1], 1), along_z(got[-1], -1)
        if tick == 0:
            near = after(near, got[2], got[-2])
            got[2] = after(got[2], cache, text_keys, text_values)
            weight_other = join_halves(info, near, across_cfg(near), depth)
        got[3], got[-3] = along_z(got[2], 1), along_z(got[-2], -1)
        if tick:
            ahead, behind = cut(got[2], got[-2], (0, SPLIT), (SPLIT, chunk), [normed])
            got[4] = [along_z(ahead, 2), along_z(behind, -2)]
        mixed, accs, others = [], [], []

        def attend_group(pieces, tokens):
            others.append(project(pieces, weight_other, tokens))
            for part in (project(pieces, weight_own), across_x(others[-1])):
                mixed.append(part)
                accs.append(
                    attend_stale(
                        tick, info, patch_order, part, cache, text_keys, text_values, fresh
                    )
                )

        attend_group([got[hops] for hops in GROUPS[0]], ())
        if tick == 0:
            rows, weight = cut(got[3], got[-3], (HEAD, HEAD + chunk), (0, HEAD), [accs[0], others[0]])
            got[4] = [along_z(rows, 1)]
            final = along_z(weight, -1)
            main = stack_weights([got[hops] for hops in HOPS[:-1]], weight)
            out_weights = (main, final, across_cfg(main), across_cfg(final))
            waited = (accs[1], main)
        else:
            waited = (accs[1],)
        attend_group([got[hops] for hops in GROUPS[1][:-1]] + got[4], waited)
        attended, *fresh = attend_fresh(info, mixed, accs, chunk, tick + 1 < TICKS)
        attended = lax.all_to_all(attended, "patch", 0, 0, axis_index_groups=columns)
        partial, flip = out_project(info, attended, out_weights, hidden, mods[tick])
        velocity, updated = finish(partial, across_x(flip), final_mods[tick], weight_final)
        outgoing = embed(
            tick,
            info,
            guidance,
            velocity,
            across_cfg(velocity),
            arrived if tick else latent,
            weight_embed,
            positions[tick],
            updated,
        )
        arrived = between(outgoing, around, 0)
    hidden_out, latent_out = unpack(arrived, width, channels)
    return (hidden_out[None, None], latent_out[None])


def solution(mesh):
    placed = (
        P("cfg", "section", "patch", None),
        P("section", "patch", None),
        P("cfg", "section", None, None, "patch"),
        P("cfg", "section", None, None, "patch"),
        P("section", None, None, "patch"),
        P("section", "patch", None),
        P("section", None, None, None),
        P(),
        P(),
        P(),
        P(None, "patch", None),
        P(),
        P(),
        P(),
    )
    return jax.shard_map(
        on_device,
        mesh=mesh,
        in_specs=placed,
        out_specs=(P("cfg", "section", "patch", None), P("section", "patch", None)),
        check_vma=False,
    )
```

```python
import math

import jax
import jax.numpy as jnp
from jax import lax
from jax.experimental import pallas as pl
from jax.experimental.pallas import tpu as pltpu
from jax.sharding import PartitionSpec as P

HEAD = 64
NT = 28
TICKS = 2
EPSILON = 1e-06
BF = jnp.bfloat16
F32 = jnp.float32
VMEM_LIMIT = 20 * 1024 * 1024
Q_SCALE = math.log2(math.e) / math.sqrt(HEAD)
GROUPS = ((0, 1, -1, 2), (-2, 3, -3, 4))
HOPS = (0, 1, 2, 3, -3, -2, -1, 4)
LANES = 128
TEXT_PAD = 384


def params():
    return pltpu.CompilerParams(vmem_limit_bytes=VMEM_LIMIT)


def cost(flops, moved, exps=0):
    return pl.CostEstimate(flops=int(flops), bytes_accessed=int(moved), transcendentals=int(exps))


def sigma_of(time_level):
    frac = 1.0 - time_level.astype(F32) / NT
    return 3.0 * frac / (1.0 + 2.0 * frac)


def normalize(values):
    center = values - jnp.mean(values, axis=-1, keepdims=True)
    return center / jnp.sqrt(jnp.mean(center * center, axis=-1, keepdims=True) + EPSILON)


def on_whole(kernel, outs, args, scalars, estimate, name, scratch=(), tokens=()):
    vmem = pl.BlockSpec(memory_space=pltpu.VMEM)
    used, waited = len(args), len(tokens)

    def body(*refs):
        kernel(*refs[:used], *refs[used + waited :])

    return pl.pallas_call(
        body,
        out_shape=[jax.ShapeDtypeStruct(shape, dtype) for shape, dtype in outs],
        in_specs=[pl.BlockSpec(memory_space=pltpu.SMEM)] * scalars
        + [vmem] * (used - scalars)
        + [pl.BlockSpec(memory_space=pl.ANY)] * waited,
        out_specs=[vmem] * len(outs),
        scratch_shapes=list(scratch),
        compiler_params=params(),
        cost_estimate=estimate,
        name=name,
    )(*args, *tokens)


def after(value, *tokens):
    anywhere = pl.BlockSpec(memory_space=pl.ANY)
    return pl.pallas_call(
        lambda *refs: None,
        out_shape=jax.ShapeDtypeStruct(value.shape, value.dtype),
        in_specs=[anywhere] * (1 + len(tokens)),
        out_specs=anywhere,
        input_output_aliases={0: 0},
        compiler_params=params(),
        cost_estimate=cost(0, 0),
        name="after",
    )(value, *tokens)


def cut(left, right, rows_left, rows_right, tokens):
    width = left.shape[1]

    def kernel(left_ref, right_ref, *outs):
        for ref, rows, out in zip((left_ref, right_ref), (rows_left, rows_right), outs):
            out[...] = ref[rows[0] : rows[1]]

    return on_whole(
        kernel,
        [((rows[1] - rows[0], width), BF) for rows in (rows_left, rows_right)],
        [left, right],
        0,
        cost(0, 400 * width),
        "cut",
        tokens=tokens,
    )


def modulate(hidden, shift, scale):
    return (normalize(hidden) * (1.0 + scale) + shift).astype(BF)


def norm_first(info, hidden, mod_table, out_weight):
    rows, width = hidden.shape
    vmem = pl.BlockSpec(memory_space=pltpu.VMEM)

    def kernel(info_ref, hidden_ref, mod_ref, weight_ref, out_ref):
        out_ref[:HEAD] = jnp.where(info_ref[1] == 0, weight_ref[:HEAD], weight_ref[HEAD:])
        out_ref[HEAD:] = modulate(hidden_ref[...], mod_ref[0, 0:1], mod_ref[0, 1:2])

    return pl.pallas_call(
        kernel,
        out_shape=jax.ShapeDtypeStruct((HEAD + rows, width), BF),
        grid_spec=pltpu.PrefetchScalarGridSpec(
            num_scalar_prefetch=1,
            grid=(1,),
            in_specs=[vmem, pl.BlockSpec((1, 3, width), lambda i, nf: (nf[3], 0, 0)), vmem],
            out_specs=vmem,
        ),
        compiler_params=params(),
        cost_estimate=cost(10 * rows * width, 6 * rows * width),
        name="norm_first",
    )(info, hidden, mod_table, out_weight)


def select_half(info, weight, reach, token):
    planes, width, lanes = weight.shape

    def kernel(info_ref, weight_ref, out_ref):
        out_ref[...] = jnp.where(
            info_ref[1] == 0, weight_ref[:, :reach], weight_ref[:, width - reach :]
        )

    return on_whole(
        kernel,
        [((planes, reach, lanes), BF)],
        [info, weight],
        1,
        cost(0, 8 * planes * reach * lanes),
        "select_half",
        tokens=[token],
    )[0]


def stack_weights(pieces, token):
    count = len(pieces)
    width = pieces[0].shape[1]

    def kernel(*refs):
        for at, ref in enumerate(refs[:-1]):
            refs[-1][at * HEAD : (at + 1) * HEAD] = ref[:HEAD]

    return on_whole(
        kernel,
        [((count * HEAD, width), BF)],
        pieces,
        0,
        cost(0, 4 * count * HEAD * width),
        "stack_weights",
        tokens=[token],
    )[0]


def norm_rows(hidden, mods):
    rows, width = hidden.shape[0], mods.shape[1]

    def kernel(hidden_ref, mod_ref, out_ref):
        values = hidden_ref[:, :width].astype(F32)
        out_ref[...] = modulate(values, mod_ref[0:1], mod_ref[1:2])

    return on_whole(
        kernel,
        [((rows, width), BF)],
        [hidden, mods],
        0,
        cost(10 * rows * width, 6 * rows * width),
        "norm_rows",
    )[0]


def prepare(info, order, mod_table, final_mod, pos_embed):
    width = mod_table.shape[2]
    chunk = pos_embed.shape[1]

    def kernel(info_ref, order_ref, *refs):
        for source, target in zip(refs[: 3 * TICKS], refs[3 * TICKS :]):
            target[...] = source[0]

    def spec(rows, index):
        return pl.BlockSpec((1, rows, width), lambda i, nf, od: (index(nf, od), 0, 0))

    specs, operands, outs = [], [], []
    for tick in range(TICKS):
        for table, index in (
            (mod_table, lambda nf, od, tick=tick: nf[3 + tick]),
            (final_mod, lambda nf, od, tick=tick: nf[3 + tick]),
            (pos_embed, lambda nf, od, tick=tick: od[tick]),
        ):
            specs.append(spec(table.shape[1], index))
            operands.append(table)
            outs.append(jax.ShapeDtypeStruct(table.shape[1:], table.dtype))
    found = pl.pallas_call(
        kernel,
        out_shape=outs,
        grid_spec=pltpu.PrefetchScalarGridSpec(
            num_scalar_prefetch=2,
            grid=(1,),
            in_specs=specs,
            out_specs=[pl.BlockSpec(memory_space=pltpu.VMEM)] * len(outs),
        ),
        compiler_params=params(),
        cost_estimate=cost(0, 8 * chunk * width),
        name="prepare",
    )(info, order, *operands)
    return found[0::3], found[1::3], found[2::3]


def join_halves(info, near, far, width):
    reach = near.shape[1]

    def kernel(info_ref, near_ref, far_ref, out_ref):
        first = info_ref[1] == 0
        near, far = near_ref[...], far_ref[...]
        out_ref[:, :reach] = jnp.where(first, near, far)
        out_ref[:, reach:] = jnp.where(first, far, near)[:, 2 * reach - width :]

    return on_whole(
        kernel,
        [((3, width, LANES), BF)],
        [info, near, far],
        1,
        cost(0, 6 * width * LANES),
        "join_halves",
    )[0]


def head_scale(values, factor):
    lane = lax.broadcasted_iota(jnp.int32, values.shape, 1)
    square = values * values
    low = jnp.sum(jnp.where(lane < HEAD, square, 0.0), axis=1, keepdims=True)
    high = jnp.sum(jnp.where(lane < HEAD, 0.0, square), axis=1, keepdims=True)
    total = jnp.where(lane < HEAD, low, high)
    return values * (factor / jnp.sqrt(total * (1.0 / HEAD) + EPSILON))


def project(pieces, weight, tokens=()):
    count = len(pieces)
    width = pieces[0].shape[1]
    rows = [piece.shape[0] - HEAD * (piece.shape[0] > HEAD) for piece in pieces]
    total = sum(rows)

    def kernel(*refs):
        piece_refs, (weight_ref, out_ref, gathered) = refs[:count], refs[count:]
        for at, ref in enumerate(piece_refs):
            start = sum(rows[:at])
            gathered[start : start + rows[at], :] = ref[ref.shape[0] - rows[at] :].astype(F32)
        mixed = jnp.dot(
            gathered[...].astype(BF),
            jnp.concatenate([weight_ref[at] for at in range(3)], axis=1),
            preferred_element_type=F32,
        )
        out_ref[:, 0:LANES] = head_scale(mixed[:, 0:LANES], Q_SCALE).astype(BF)
        out_ref[:, LANES : 2 * LANES] = head_scale(mixed[:, LANES : 2 * LANES], 1.0).astype(BF)
        out_ref[:, 2 * LANES :] = mixed[:, 2 * LANES :].astype(BF)

    return on_whole(
        kernel,
        [((total, 3 * LANES), BF)],
        [*pieces, weight],
        0,
        cost(2 * total * width * 3 * LANES, 6 * LANES * width + 2 * total * width),
        "project",
        [pltpu.VMEM((total, width), F32)],
        tokens,
    )[0]


def masked_queries(queries):
    lane = lax.broadcasted_iota(jnp.int32, queries.shape, 1)
    zero = jnp.zeros_like(queries)
    return jnp.where(lane < HEAD, queries, zero), jnp.where(lane < HEAD, zero, queries)


def weigh(query, keys, values):
    scores = lax.dot_general(
        query, keys, (((1,), (1,)), ((), ())), preferred_element_type=F32
    )
    return jnp.dot(jnp.exp2(scores).astype(BF), values, preferred_element_type=F32)


def with_ones(values):
    return jnp.concatenate([values, jnp.ones(values.shape, BF)], axis=1)


def attend_stale(tick, info, order, mixed, cache, text_keys, text_values, fresh):
    rows = mixed.shape[0]
    patches, patch_rows = cache.shape[1:3]
    blocks = patches - 1 - tick
    extra = len(fresh)

    def kernel(info_ref, order_ref, mixed_ref, cache_ref, text_key_ref, text_value_ref, *rest):
        fresh_refs, acc_ref = rest[:extra], rest[extra]
        places = [
            order_ref[lax.rem(2 * patches + tick - info_ref[2] + block, patches)]
            for block in range(blocks)
        ]
        queries = masked_queries(mixed_ref[:, 0:LANES])
        loads = [lambda: (text_key_ref[...], text_value_ref[...])]
        if extra:
            loads.append(lambda: (fresh_refs[0][...], with_ones(fresh_refs[1][...])))
        for at in places:
            loads.append(lambda at=at: (cache_ref[0, at], with_ones(cache_ref[1, at])))
        totals = [0.0, 0.0]
        for at in range(0, len(loads), 2):
            sets = [load() for load in loads[at : at + 2]]
            key_set = jnp.concatenate([each[0] for each in sets], axis=0)
            value_set = jnp.concatenate([each[1] for each in sets], axis=0)
            for head, query in enumerate(queries):
                totals[head] = totals[head] + weigh(query, key_set, value_set)
        for head, total in enumerate(totals):
            acc_ref[head * rows : (head + 1) * rows] = total

    total_keys = blocks * patch_rows + TEXT_PAD + (patch_rows if extra else 0)
    vmem = pl.BlockSpec(memory_space=pltpu.VMEM)
    smem = pl.BlockSpec(memory_space=pltpu.SMEM)
    return pl.pallas_call(
        kernel,
        out_shape=jax.ShapeDtypeStruct((2 * rows, 2 * LANES), F32),
        in_specs=[smem, smem] + [vmem] * (4 + extra),
        out_specs=vmem,
        compiler_params=params(),
        cost_estimate=cost(
            4 * 2 * rows * total_keys * 256, 4 * LANES * total_keys, 2 * rows * total_keys
        ),
        name="attend_stale",
    )(info, order, mixed, cache, text_keys, text_values, *fresh)


def attend_fresh(place, mixed, accs, chunk, keep):
    count = len(mixed)
    sizes = [array.shape[0] for array in mixed]
    total = sum(sizes)
    hops = [k for group in GROUPS for k in group]
    steps = len(hops)

    def kernel(place_ref, *refs):
        mixed_refs, acc_refs = refs[:count], refs[count : 2 * count]
        out_ref, keys_ref, values_ref = refs[2 * count :]
        at = 0
        for ref, size in zip(mixed_refs, sizes):
            keys_ref[at : at + size] = ref[:, LANES : 2 * LANES]
            values_ref[at : at + size] = ref[:, 2 * LANES :]
            at += size
        value_block = with_ones(values_ref[...])
        everyone = jnp.concatenate([ref[:, 0:LANES] for ref in mixed_refs], axis=0)
        sums = []
        for head, query in enumerate(masked_queries(everyone)):
            before = [
                acc_ref[head * size : (head + 1) * size] for acc_ref, size in zip(acc_refs, sizes)
            ]
            sums.append(
                jnp.concatenate(before, axis=0) + weigh(query, keys_ref[...], value_block)
            )
        lane = lax.broadcasted_iota(jnp.int32, (total, LANES), 1)
        top = jnp.where(lane < HEAD, sums[0][:, :LANES], sums[1][:, :LANES])
        bottom = jnp.where(lane < HEAD, sums[0][:, LANES:], sums[1][:, LANES:])
        result = top / bottom
        result = jnp.where(place_ref[1] == 0, result, pltpu.roll(result, HEAD, 1))
        row, hop_at = 0, 0
        for at, size in enumerate(sizes):
            for index in range(size // chunk):
                target = lax.rem(place_ref[0] + steps - hops[hop_at + index], steps)
                out_ref[target, at % 2] = result[row : row + chunk].astype(BF)
                row += chunk
            if at % 2:
                hop_at += size // chunk

    pair = [((total, LANES), BF)] * 2
    return on_whole(
        kernel,
        [((steps, 2, chunk, LANES), BF)] + (pair if keep else []),
        [place, *mixed, *accs],
        1,
        cost(4 * total * 2 * total * 256, 8 * total * 1024, 2 * total * total),
        "attend_fresh",
        [] if keep else [pltpu.VMEM(*each) for each in pair],
    )


def out_project(info, attended, weights, hidden, mods):
    sources, _, chunk, _ = attended.shape
    width = mods.shape[1]

    def kernel(info_ref, attended_ref, *refs):
        weight_refs, (hidden_ref, mod_ref, sum_ref, flip_ref) = refs[:4], refs[4:]
        lane = lax.broadcasted_iota(jnp.int32, (2 * chunk, LANES), 1)
        gate = mod_ref[2:3]
        blocks = []
        for hop in HOPS:
            at = lax.rem(info_ref[0] + sources - hop, sources)
            blocks.append(
                jnp.concatenate([attended_ref[at, side].astype(F32) for side in range(2)], axis=0)
            )
        halves = ([], [])
        for even, odd in zip(blocks[::2], blocks[1::2]):
            halves[0].append(jnp.where(lane < HEAD, even, pltpu.roll(odd, HEAD, 1)).astype(BF))
            halves[1].append(jnp.where(lane < HEAD, pltpu.roll(even, HEAD, 1), odd).astype(BF))
        sums = 0.0
        for half, (main_ref, final_ref) in zip(halves, (weight_refs[:2], weight_refs[2:])):
            whole = main_ref.shape[0] // LANES
            tail = jnp.concatenate([main_ref[whole * LANES :], final_ref[...]], axis=0)
            sums = sums + jnp.dot(
                jnp.concatenate(half[:whole], axis=1),
                main_ref[: whole * LANES],
                preferred_element_type=F32,
            )
            sums = sums + jnp.dot(half[whole], tail, preferred_element_type=F32)
        sum_ref[...] = hidden_ref[:, :width].astype(F32) + gate * sums[:chunk]
        flip_ref[...] = (gate * sums[chunk:]).astype(BF)

    return on_whole(
        kernel,
        [((chunk, width), F32), ((chunk, width), BF)],
        [info, attended, *weights, hidden, mods],
        1,
        cost(4 * chunk * sources * LANES * width, 4 * sources * HEAD * width),
        "out_project",
    )


def finish(partial, recv, final_mods, final_weight):
    rows, width = partial.shape
    channels = final_weight.shape[0]

    def kernel(partial_ref, recv_ref, final_ref, weight_ref, vel_ref, out_ref):
        updated = partial_ref[...] + recv_ref[...].astype(F32)
        out_ref[...] = updated.astype(BF)
        normed = modulate(updated, final_ref[0:1], final_ref[1:2])
        vel_ref[...] = lax.dot_general(
            normed, weight_ref[...], (((1,), (1,)), ((), ())), preferred_element_type=F32
        )

    return on_whole(
        kernel,
        [((rows, channels), F32), ((rows, width), BF)],
        [partial, recv, final_mods, final_weight],
        0,
        cost(20 * rows * width, 16 * rows * width),
        "finish",
    )


def embed(tick, info, guidance, velocity, partner, latent, weight, positions, updated):
    rows, width = positions.shape
    start = latent.shape[1] - 2 * LANES

    def kernel(info_ref, guide_ref, vel_ref, partner_ref, latent_ref, weight_ref, pos_ref, updated_ref, out_ref):
        first = info_ref[1] == 0
        last = info_ref[5] == 1
        level = jnp.full((rows, LANES), info_ref[3 + tick], jnp.int32)
        guide = jnp.full((rows, LANES), guide_ref[0], jnp.int32).astype(F32) / 64.0
        velocity, partner = vel_ref[...], partner_ref[...]
        conditional = jnp.where(first, velocity, partner)
        unconditional = jnp.where(first, partner, velocity)
        guided = unconditional + guide * (conditional - unconditional)
        latent = latent_ref[:, start : start + LANES].astype(F32)
        latent = latent + latent_ref[:, start + LANES :].astype(F32)
        moved = latent + (sigma_of(level + 1) - sigma_of(level)) * guided
        embedded = jnp.dot(moved.astype(BF), weight_ref[...], preferred_element_type=F32)
        embedded = (embedded + pos_ref[...].astype(F32)).astype(BF)
        out_ref[:, :width] = jnp.where(last, embedded, updated_ref[...])
        latent = jnp.where(last, moved, latent)
        high = latent.astype(BF)
        out_ref[:, width : width + LANES] = high
        out_ref[:, width + LANES :] = (latent - high.astype(F32)).astype(BF)

    return on_whole(
        kernel,
        [((rows, width + 2 * LANES), BF)],
        [info, guidance, velocity, partner, latent, weight, positions, updated],
        2,
        cost(2 * rows * width * LANES, 10 * rows * width),
        "embed",
    )[0]


def unpack(arrived, width, channels):
    rows = arrived.shape[0]

    def kernel(arrived_ref, hidden_ref, latent_ref):
        hidden_ref[...] = arrived_ref[:, :width].astype(F32)
        latent = arrived_ref[:, width : width + LANES].astype(F32)
        latent = latent + arrived_ref[:, width + LANES :].astype(F32)
        latent_ref[...] = latent[:, :channels]

    return on_whole(
        kernel,
        [((rows, width), F32), ((rows, channels), F32)],
        [arrived],
        0,
        cost(rows * width, 6 * rows * width),
        "unpack",
    )


def on_device(
    hidden_in,
    latent_in,
    kv_cache,
    text_kv,
    qkv_weight,
    out_weight,
    mod_table,
    final_mod,
    final_weight,
    embed_weight,
    pos_embed,
    patch_order,
    step_index,
    guidance,
):
    sections = lax.axis_size("section")
    members = lax.axis_size("patch")
    ring = members // 2
    section = lax.axis_index("section")
    branch = lax.axis_index("cfg")
    place = lax.axis_index("patch") // 2

    def along_z(value, hops):
        pairs = [(at, (at + 2 * hops) % members) for at in range(members)]
        return lax.ppermute(value, "patch", pairs)

    def across_x(value):
        return lax.ppermute(value, "patch", [(at, at ^ 1) for at in range(members)])

    def across_cfg(value):
        return lax.ppermute(value, "cfg", [(0, 1), (1, 0)])

    def between(value, moves, flip):
        pairs = [
            (source * members + at, target * members + (at ^ flip))
            for source, target in moves
            for at in range(members)
        ]
        return lax.ppermute(value, ("section", "patch"), pairs)

    last = sections - 1
    around = [(at, (at + 1) % sections) for at in range(sections)]
    columns = [[2 * z + x for z in range(ring)] for x in range(2)]
    chunk, width = hidden_in.shape[2:]
    channels = latent_in.shape[2]
    spare = ((0, 0), (0, LANES - channels))
    latent = jnp.pad(latent_in[0], ((0, 0), (0, 2 * LANES - channels)))
    weight_final = jnp.pad(jnp.transpose(final_weight), (spare[1], spare[0]))
    weight_embed = jnp.pad(embed_weight, (spare[1], spare[0]))
    patch_rows = chunk * members
    depth = qkv_weight.shape[1]

    info = jnp.stack(
        [
            place,
            branch,
            section,
            step_index[0] + (last - section >= sections).astype(jnp.int32),
            step_index[0] + (last + 1 - section >= sections).astype(jnp.int32),
            (section == last).astype(jnp.int32),
        ]
    ).astype(jnp.int32)
    hidden = hidden_in[0, 0]
    normed = norm_first(info, hidden, mod_table[0], out_weight[0])
    fresh = ()
    for tick in range(TICKS):
        if tick:
            hidden = arrived
            normed = norm_rows(hidden, mods[tick])
        got = {0: normed, 1: along_z(normed, 1), -1: along_z(normed, -1)}
        if tick == 0:
            weight_own = jnp.transpose(qkv_weight[0], (1, 0, 2))
            reach = (depth // 2 + LANES - 1) // LANES * LANES
            half = select_half(info, weight_own, reach, normed)
            mods, final_mods, positions = prepare(
                info, patch_order, mod_table[0], final_mod, pos_embed
            )
            got[1] = after(got[1], half, mods[0])
            near = across_x(half)
            cache = jnp.transpose(kv_cache[0, 0], (1, 0, 2)).reshape(2, -1, patch_rows, LANES)
            text = text_kv[0, 0]
            pad = ((0, TEXT_PAD - text.shape[0]), (0, 0))
            text_keys = jnp.pad(text[:, 0], pad)
            text_values = jnp.pad(
                jnp.concatenate([text[:, 1], jnp.ones((text.shape[0], LANES), BF)], axis=1), pad
            )
        got[2], got[-2] = along_z(got[1], 1), along_z(got[-1], -1)
        if tick == 0:
            near = after(near, got[2], got[-2])
            got[2] = after(got[2], cache, text_keys, text_values)
            weight_other = join_halves(info, near, across_cfg(near), depth)
        got[3], got[-3] = along_z(got[2], 1), along_z(got[-2], -1)
        if tick:
            got[4] = [along_z(got[2], 2)]
        mixed, accs, others = [], [], []

        def attend_group(pieces, tokens):
            others.append(project(pieces, weight_other, tokens))
            for part in (project(pieces, weight_own), across_x(others[-1])):
                mixed.append(part)
                accs.append(
                    attend_stale(
                        tick, info, patch_order, part, cache, text_keys, text_values, fresh
                    )
                )

        attend_group([got[hops] for hops in GROUPS[0]], ())
        if tick == 0:
            rows, weight = cut(got[3], got[-3], (HEAD, HEAD + chunk), (0, HEAD), [accs[0], others[0]])
            got[4] = [along_z(rows, 1)]
            final = along_z(weight, -1)
            main = stack_weights([got[hops] for hops in HOPS[:-1]], weight)
            out_weights = (main, final, across_cfg(main), across_cfg(final))
            waited = (accs[1], main)
        else:
            waited = (accs[1],)
        attend_group([got[hops] for hops in GROUPS[1][:-1]] + got[4], waited)
        attended, *fresh = attend_fresh(info, mixed, accs, chunk, tick + 1 < TICKS)
        attended = lax.all_to_all(attended, "patch", 0, 0, axis_index_groups=columns)
        partial, flip = out_project(info, attended, out_weights, hidden, mods[tick])
        velocity, updated = finish(partial, across_x(flip), final_mods[tick], weight_final)
        outgoing = embed(
            tick,
            info,
            guidance,
            velocity,
            across_cfg(velocity),
            arrived if tick else latent,
            weight_embed,
            positions[tick],
            updated,
        )
        arrived = between(outgoing, around, 0)
    hidden_out, latent_out = unpack(arrived, width, channels)
    return (hidden_out[None, None], latent_out[None])


def solution(mesh):
    placed = (
        P("cfg", "section", "patch", None),
        P("section", "patch", None),
        P("cfg", "section", None, None, "patch"),
        P("cfg", "section", None, None, "patch"),
        P("section", None, None, "patch"),
        P("section", "patch", None),
        P("section", None, None, None),
        P(),
        P(),
        P(),
        P(None, "patch", None),
        P(),
        P(),
        P(),
    )
    return jax.shard_map(
        on_device,
        mesh=mesh,
        in_specs=placed,
        out_specs=(P("cfg", "section", "patch", None), P("section", "patch", None)),
        check_vma=False,
    )
```
